256 devices in a mesh: replica: 16 (over x, y), tensor: 16 (over z, core).
Axes of the slice: x: 4, y: 4, z: 8, core: 2. Of those that a mesh axis runs over, the one named last changes fastest.
Arguments:
- momentum: float32 [16, 1024, 8192], P('replica', None, 'tensor'), may hold values from -6 to 6
- gradient: bfloat16 [16, 1024, 8192], P('replica', None, 'tensor'), may hold values from -110 to 110
- kept_freq: int32 [16, 16, 128, 32], P('replica', None, 'tensor'), may hold values from 0 to 4095, all different within a row
- clip_flag: int32 [16], P('replica'), may hold values from 0 to 1
Outputs:
- new_momentum: float32 [16, 1024, 8192], P('replica', None, 'tensor')
- update: float32 [1024, 8192], P(None, 'tensor')
The draws below stay inside these ranges and needn't reach their ends.
Inputs may be any that keep to these rules, and one draw needn't show every extreme that they name: `kept_freq`: within one block the 32 frequencies of a replica differ.
All inputs are finite; a program needn't handle non-finite values.
Results may differ from the reference program's by a relative error of at most 0.0003.
Values sent between devices are 32-bit elements; how exact they have to be, the bound alone decides.
No kernel may reach another device: no remote copies, remote signals or barrier semaphores. Data moves between devices by JAX's collectives and lax.ppermute only.
A program may use at most 64 MiB of HBM per device.

```python
import math
import jax
import jax.numpy as jnp
from jax import lax

D = 8192
KVDIM = 1024
GROUP = 64
TOPK = 32
N_REPLICA = 16


def draw_gradient(key, part):
    key = jax.random.fold_in(key, 7)
    key_noise, key_row, key_col = jax.random.split(key, 3)
    noise = jax.random.normal(key_noise, (N_REPLICA, KVDIM, D), jnp.float32)
    noise = jnp.clip(noise, -6.0, 6.0)
    row_scale = jnp.exp(jax.random.uniform(key_row, (N_REPLICA, KVDIM, 1), jnp.float32) * math.log(10.0))
    col_scale = jnp.exp(jax.random.uniform(key_col, (1, 1, D), jnp.float32) * math.log(10.0))
    rep_pos = jnp.arange(N_REPLICA, dtype=jnp.float32) / max(N_REPLICA - 1, 1)
    col_pos = jnp.arange(D, dtype=jnp.float32) / D
    rising = jnp.exp(math.log(3.0) * rep_pos)[:, None, None] * jnp.exp(math.log(3.0) * col_pos)[None, None, :]
    return (0.02 * noise * row_scale * col_scale * rising).astype(jnp.bfloat16)


def plant(values, own_key, smallest, largest):
    index_at = [jax.random.randint(jax.random.fold_in(own_key, axis), (), 0, length) for axis, length in enumerate(values.shape)]
    main_axis = values.shape.index(max(values.shape))
    neighbour = index_at[:main_axis] + [(index_at[main_axis] + 1) % values.shape[main_axis]] + index_at[main_axis + 1:]
    return values.at[tuple(index_at)].set(smallest).at[tuple(neighbour)].set(largest)


def shard_levels(key, extent, shards, smallest, largest):
    factor_of, own = 1.0, jax.random.fold_in(key, 6)
    for position, blocks in shards:
        steps = jnp.exp(jax.random.uniform(jax.random.fold_in(own, position), (blocks,), jnp.float32, smallest / len(shards), largest / len(shards)))
        factor_of = factor_of * jnp.repeat(steps, extent[position] // blocks).reshape([-1 if axis == position else 1 for axis in range(len(extent))])
    return factor_of


def distinct(stream_key, rows, number_of, top, lift):
    sequence = jax.random.permutation(jax.random.fold_in(stream_key, 1), number_of)
    favour = sequence
    for power in range(3):
        favour = favour * favour // number_of
    favour = favour * lift // number_of
    lots = jax.random.randint(jax.random.fold_in(stream_key, 2), (rows, number_of), 0, 4096) + favour
    holders = jax.random.permutation(jax.random.fold_in(stream_key, 3), rows)[jnp.arange(number_of) % rows]
    lots = jnp.where(jnp.arange(rows)[:, None] == holders[None, :], 1 << 14, lots)
    priority = lots * number_of + jnp.arange(number_of)
    return lax.top_k(priority.astype(jnp.int32), top)[1].astype(jnp.int32)


def normal_values(key, shape, scale, limit, cuts=(), kind=jnp.bfloat16):
    gain = shard_levels(key, shape, cuts, -0.22, 0.18) if cuts else 1.0
    result = jax.random.normal(key, shape, jnp.float32) * scale * gain
    return jnp.minimum(jnp.maximum(result, -limit), limit).astype(kind)


def setup_inputs(seed: int = 0) -> dict:
    keys = jax.random.split(jax.random.key(seed), 5)
    return {
        "momentum": normal_values(keys[0], (N_REPLICA, KVDIM, D), 1.0, 6.0, ((0, 16), (2, 16)), jnp.float32),
        "gradient": draw_gradient(jax.random.fold_in(keys[4], 71), 0),
        "kept_freq": distinct(keys[2], N_REPLICA * (KVDIM // GROUP) * (D // GROUP), GROUP * GROUP, TOPK, 0).reshape((N_REPLICA, KVDIM // GROUP, D // GROUP, TOPK)),
        "clip_flag": plant(jax.random.randint(keys[3], (N_REPLICA,), 0, 2), jax.random.fold_in(keys[3], 1), 0, 1).astype(jnp.int32),
    }


CLIP_RMS = 0.5
DECAY = 0.9

def cosine_table(width):
    freq = jnp.arange(width, dtype=jnp.float32)[:, None]
    place = jnp.arange(width, dtype=jnp.float32)[None, :]
    weight = jnp.where(freq == 0, 1.0, 2.0) / width
    return (jnp.sqrt(weight) * jnp.cos(math.pi * (2.0 * place + 1.0) * freq / (2.0 * width))).astype(jnp.float32)

def forward(field, table):
    width = table.shape[0]
    blocks = field.reshape(field.shape[0] // width, width, field.shape[1] // width, width)
    rows_done = jnp.einsum('ap,ipjq->iajq', table, blocks, precision=lax.Precision.HIGHEST)
    return jnp.einsum('bq,iajq->ijab', table, rows_done, precision=lax.Precision.HIGHEST)

def inverse(coef, table):
    width = table.shape[0]
    rows_done = jnp.einsum('ap,ijab->ipjb', table, coef, precision=lax.Precision.HIGHEST)
    full = jnp.einsum('bq,ipjb->ipjq', table, rows_done, precision=lax.Precision.HIGHEST)
    return full.reshape(coef.shape[0] * width, coef.shape[1] * width)

def spread(values, freq, cells):
    brows, bcols = (freq.shape[-3], freq.shape[-2])
    row_ids = jnp.arange(brows, dtype=jnp.int32)[:, None, None]
    col_ids = jnp.arange(bcols, dtype=jnp.int32)[None, :, None]
    base = jnp.zeros((brows, bcols, cells), jnp.float32)
    return base.at[row_ids, col_ids, freq].add(values)

def reference(momentum, gradient, kept_freq, clip_flag):
    table = cosine_table(GROUP)
    cells = GROUP * GROUP
    wide = gradient.astype(jnp.float32)
    total = jnp.sum(wide * wide)
    rms = jnp.sqrt(total / (N_REPLICA * KVDIM * D))
    factor = jnp.minimum(jnp.float32(1.0), CLIP_RMS / (rms + 1e-06))
    scales = jnp.where(clip_flag == 1, factor, jnp.float32(1.0)).astype(jnp.float32)

    def one(pack):
        mom, grad, freq, scale = pack
        accum = DECAY * mom + scale * grad.astype(jnp.float32)
        coef = forward(accum, table)
        flat = coef.reshape(coef.shape[0], coef.shape[1], cells)
        kept = jnp.take_along_axis(flat, freq, axis=2)
        sparse = spread(kept, freq, cells).reshape(coef.shape)
        return (accum - inverse(sparse, table), kept)
    new_momentum, kept_all = lax.map(one, (momentum, gradient, kept_freq, scales))

    def add_one(pooled, pack):
        kept, freq = pack
        return (pooled + spread(kept, freq, cells), None)
    start = jnp.zeros((KVDIM // GROUP, D // GROUP, cells), jnp.float32)
    pooled, unused = lax.scan(add_one, start, (kept_all, kept_freq))
    pooled = (pooled / N_REPLICA).reshape(KVDIM // GROUP, D // GROUP, GROUP, GROUP)
    return (new_momentum, inverse(pooled, table))
```

```python
import math

import jax
import jax.numpy as jnp
import ml_dtypes
import numpy as np
from jax import lax
from jax.experimental import pallas as pl
from jax.experimental.pallas import tpu as pltpu
from jax.sharding import PartitionSpec as P

GROUP = 64
TOPK = 32
LANES = 128
CLIP_RMS = 0.5
DECAY = 0.9
F32 = jnp.float32
BF16 = jnp.bfloat16


def split_table(table):
    high = table.astype(ml_dtypes.bfloat16)
    low = (table - high.astype(np.float64)).astype(ml_dtypes.bfloat16)
    return high, low


def tables():
    freq = np.arange(GROUP)[:, None]
    place = np.arange(GROUP)[None, :]
    table = np.sqrt(np.where(freq == 0, 1.0, 2.0) / GROUP) * np.cos(math.pi * (2 * place + 1) * freq / (2 * GROUP))
    high, low = split_table(table)
    stacked = np.concatenate([high.T, low.T], axis=0)
    eye = np.eye(4)
    rows = np.stack(split_table(np.kron(eye, table.T)))
    cols = np.stack(split_table(np.kron(eye, table)))
    return stacked, rows, cols


def halves(x):
    high = x.astype(BF16)
    return high, (x - high.astype(F32)).astype(BF16)


def dot(a, b):
    return jnp.dot(a, b, preferred_element_type=F32)


def dot_nt(a, b):
    return lax.dot_general(a, b, (((1,), (1,)), ((), ())), preferred_element_type=F32)


def square_kernel(grad_ref, out_ref):
    @pl.when(pl.program_id(0) == 0)
    def _():
        out_ref[...] = jnp.zeros_like(out_ref)

    g = grad_ref[...].astype(F32)
    g = g * g
    g = g.reshape(-1, 8, g.shape[1]).sum(axis=0)
    part = sum(g[:, n * LANES:(n + 1) * LANES] for n in range(g.shape[1] // LANES))
    for n in range(out_ref.shape[0]):
        out_ref[n] += part


def table_rows(freq, stacked):
    a = lax.shift_right_logical(freq, 6)
    b = lax.bitwise_and(freq, GROUP - 1)
    place = lax.broadcasted_iota(jnp.int32, (GROUP, LANES), 0)
    hot_a = jnp.where(place == a, 1.0, 0.0).astype(BF16)
    hot_b = jnp.where(place == b, 1.0, 0.0).astype(BF16)
    both = dot(stacked, jnp.concatenate([hot_a, hot_b], axis=1))
    return both[:GROUP, :LANES], both[GROUP:, :LANES], both[:GROUP, LANES:], both[GROUP:, LANES:]


def diagonal(x):
    lane = lax.broadcasted_iota(jnp.int32, x.shape, 1)
    zero = jnp.zeros_like(x)
    return jnp.concatenate([jnp.where(lane // TOPK == m, x, zero) for m in range(4)], axis=0)


def kept_kernel(flag_ref, mom_ref, grad_ref, freq_ref, square_ref, stacked_ref, out_ref):
    step = pl.program_id(0)
    flag = (flag_ref[0] == 1).astype(F32)
    stacked = stacked_ref[...]
    copies = out_ref.shape[0]
    chunks = freq_ref.shape[0]
    freqs = freq_ref[pl.ds(pl.multiple_of(step * 8, 8), 8), :]
    us, vs = [], []
    for s in range(8):
        row, col = s // 2, s % 2
        freq = freqs[s:s + 1, :]
        ah, al, bh, bl = table_rows(freq, stacked)
        weights = jnp.concatenate([diagonal(bh), diagonal(bl)], axis=1).astype(BF16)
        x = mom_ref[row * GROUP:(row + 1) * GROUP, col * 256:(col + 1) * 256]
        g = grad_ref[row * GROUP:(row + 1) * GROUP, col * 256:(col + 1) * 256]
        xh, xl = halves(x)
        y = dot(jnp.concatenate([xh, xl, g], axis=0), weights)
        y = y[:, :LANES] + y[:, LANES:]
        a = ah + al
        km = jnp.sum((y[:GROUP] + y[GROUP:2 * GROUP]) * a, axis=0, keepdims=True)
        kg = jnp.sum(y[2 * GROUP:] * a, axis=0, keepdims=True)
        us.append(DECAY * km + (1.0 - flag) * kg)
        vs.append(flag * kg)
    u = jnp.concatenate(us, axis=0)
    v = jnp.concatenate(vs, axis=0)
    f = freqs.astype(F32)
    at = pl.multiple_of(step * 8, 8)
    for n in range(copies):
        out_ref[n, pl.ds(at, 8), :] = u
        out_ref[n, pl.ds(chunks + at, 8), :] = v
        out_ref[n, pl.ds(2 * chunks + at, 8), :] = f

    @pl.when(step == 0)
    def _():
        total = jnp.sum(square_ref[...], axis=0)
        for n in range(copies):
            out_ref[n, 3 * chunks:, :] = total


def update_kernel(count, flag_ref, mom_ref, grad_ref, own_ref, all_ref, stacked_ref, rows_ref, cols_ref, mom_out, update_out,
                  lists_a, lists_b, lists_h, lists_l, pooled):
    step = pl.program_id(0)
    replicas = all_ref.shape[0]
    chunks = (all_ref.shape[1] - 8) // 3
    stacked = stacked_ref[...]
    total = jnp.sum(all_ref[:, 3 * chunks:, :], axis=0)
    total = jnp.sum(total, axis=(0, 1), keepdims=True)
    rms = jnp.sqrt(total * (1.0 / count))
    factor = jnp.minimum(jnp.float32(1.0), CLIP_RMS / (rms + 1e-06))
    flag = (flag_ref[0] == 1).astype(F32)
    scale = flag * factor + (1.0 - flag)
    at = pl.multiple_of(step * 8, 8)

    lane = lax.broadcasted_iota(jnp.int32, (8, LANES), 1) // TOPK
    for group in range(replicas // 4):
        ks, fs = [], []
        for r in range(4 * group, 4 * group + 4):
            u = all_ref[r, pl.ds(at, 8), :]
            v = all_ref[r, pl.ds(chunks + at, 8), :]
            ks.append((u + factor * v) * (1.0 / replicas))
            fs.append(all_ref[r, pl.ds(2 * chunks + at, 8), :])
        for m in range(4):
            def regroup(xs):
                out = xs[m]
                parts = [x if r == m else pltpu.roll(x, (TOPK * (r - m)) % LANES, 1) for r, x in enumerate(xs)]
                out = parts[0]
                for r in range(1, 4):
                    out = jnp.where(lane == r, parts[r], out)
                return out
            k = regroup(ks)
            f = regroup(fs).astype(jnp.int32)
            high = k.astype(BF16).astype(F32)
            place = slice(group * LANES, (group + 1) * LANES)
            lists_a[m, :, place] = lax.shift_right_logical(f, 6)
            lists_b[m, :, place] = lax.bitwise_and(f, GROUP - 1)
            lists_h[m, :, place] = high
            lists_l[m, :, place] = k - high

    items = replicas * TOPK
    place = lax.broadcasted_iota(jnp.int32, (GROUP, items), 0)
    left = lax.broadcasted_iota(jnp.int32, (GROUP, LANES), 1) < GROUP

    def scatter(s, m):
        here = pl.ds(s, 1)
        hot_a = jnp.where(place == lists_a[m, here, :], 1.0, 0.0).astype(BF16)
        hit = place == lists_b[m, here, :]
        high = jnp.where(hit, lists_h[m, here, :], 0.0).astype(BF16)
        low = jnp.where(hit, lists_l[m, here, :], 0.0).astype(BF16)
        out = dot_nt(hot_a, jnp.concatenate([high, low], axis=0))
        return out + pltpu.roll(out, GROUP, 1)

    def block_row(row, carry):
        top = pl.ds(pl.multiple_of(row * GROUP, GROUP), GROUP)
        for col in range(2):
            s = row * 2 + col
            for pair in range(2):
                both = jnp.where(left, scatter(s, 2 * pair), scatter(s, 2 * pair + 1))
                pooled[top, col * 256 + pair * LANES:col * 256 + (pair + 1) * LANES] = both
            here = pl.ds(at + s, 1)
            freq = own_ref[pl.ds(2 * chunks + at + s, 1), :].astype(jnp.int32)
            k = own_ref[here, :] + factor * own_ref[pl.ds(chunks + at + s, 1), :]
            ah, al, bh, bl = table_rows(freq, stacked)
            wh, wl = halves((bh + bl) * k)
            wh, wl = diagonal(wh.astype(F32)).astype(BF16), diagonal(wl.astype(F32)).astype(BF16)
            ah, al = ah.astype(BF16), al.astype(BF16)
            out = dot_nt(jnp.concatenate([ah, al], axis=1), jnp.concatenate([wh, wh], axis=1)) + dot_nt(ah, wl)
            wide = slice(col * 256, (col + 1) * 256)
            mom_out[top, wide] = DECAY * mom_ref[top, wide] + scale * grad_ref[top, wide].astype(F32) - out
        return carry

    lax.fori_loop(0, 4, block_row, 0)

    ph, plow = halves(pooled[...])
    rh, rl = rows_ref[0], rows_ref[1]
    y = dot(rh, ph) + dot(rh, plow) + dot(rl, ph)
    ch, cl = cols_ref[0], cols_ref[1]
    for col in range(2):
        wide = slice(col * 256, (col + 1) * 256)
        yh, yl = halves(y[:, wide])
        update_out[:, wide] = dot(yh, ch) + dot(yl, ch) + dot(yh, cl)


def full(shape):
    return pl.BlockSpec(shape, lambda i: (0,) * len(shape))


def body(momentum, gradient, kept_freq, clip_flag):
    replicas, tensors = lax.axis_size("replica"), lax.axis_size("tensor")
    mom, grad = momentum[0], gradient[0]
    rows, cols = mom.shape
    steps = rows // 256
    chunks = rows // GROUP * cols // GROUP * TOPK // LANES
    stacked, row_table, col_table = (jnp.asarray(t) for t in tables())
    freq = kept_freq[0].reshape(chunks, LANES)
    band = pl.BlockSpec((256, cols), lambda i: (i, 0))
    scalar = pl.BlockSpec(memory_space=pltpu.SMEM)
    limit = pltpu.CompilerParams(vmem_limit_bytes=40 * 1024 * 1024)

    squares = pl.pallas_call(
        square_kernel,
        grid=(steps,),
        in_specs=[band],
        out_specs=full((tensors, 8, LANES)),
        out_shape=jax.ShapeDtypeStruct((tensors, 8, LANES), F32),
        compiler_params=limit,
    )(grad)
    squares = lax.all_to_all(squares, "tensor", 0, 0)

    message = pl.pallas_call(
        kept_kernel,
        grid=(steps,),
        in_specs=[scalar, band, band, full(freq.shape), full(squares.shape), full(stacked.shape)],
        out_specs=full((replicas, 3 * chunks + 8, LANES)),
        out_shape=jax.ShapeDtypeStruct((replicas, 3 * chunks + 8, LANES), F32),
        compiler_params=limit,
    )(clip_flag, mom, grad, freq, squares, stacked)
    own = message[0]
    everyone = lax.all_to_all(message, "replica", 0, 0)

    new_mom, update = pl.pallas_call(
        lambda *refs: update_kernel(replicas * tensors * rows * cols, *refs),
        grid=(steps,),
        in_specs=[scalar, band, band, full(own.shape), full(everyone.shape), full(stacked.shape),
                  full(row_table.shape), full(col_table.shape)],
        out_specs=[band, band],
        out_shape=[jax.ShapeDtypeStruct((rows, cols), F32)] * 2,
        scratch_shapes=[pltpu.VMEM((4, 8, replicas * TOPK), t) for t in (jnp.int32, jnp.int32, F32, F32)]
        + [pltpu.VMEM((256, cols), F32)],
        compiler_params=limit,
    )(clip_flag, mom, grad, own, everyone, stacked, row_table, col_table)
    return (new_mom[None], update)


def solution(mesh):
    placed = (
        P("replica", None, "tensor"),
        P("replica", None, "tensor"),
        P("replica", None, "tensor", None),
        P("replica"),
    )
    return jax.shard_map(
        body,
        mesh=mesh,
        in_specs=placed,
        out_specs=(P("replica", None, "tensor"), P(None, "tensor")),
        check_vma=False,
    )
```

```python
import math

import jax
import jax.numpy as jnp
import ml_dtypes
import numpy as np
from jax import lax
from jax.experimental import pallas as pl
from jax.experimental.pallas import tpu as pltpu
from jax.sharding import PartitionSpec as P

GROUP = 64
TOPK = 32
LANES = 128
TILE = (512, 256)
CLIP_RMS = 0.5
DECAY = 0.9
F32 = jnp.float32
BF16 = jnp.bfloat16


def split_table(table):
    high = table.astype(ml_dtypes.bfloat16)
    low = (table - high.astype(np.float64)).astype(ml_dtypes.bfloat16)
    return high, low


def tables():
    freq = np.arange(GROUP)[:, None]
    place = np.arange(GROUP)[None, :]
    table = np.sqrt(np.where(freq == 0, 1.0, 2.0) / GROUP) * np.cos(math.pi * (2 * place + 1) * freq / (2 * GROUP))
    high, low = split_table(table)
    stacked = np.concatenate([high.T, low.T], axis=0)
    eye = np.eye(4)
    rows = np.stack(split_table(np.kron(eye, table.T)))
    cols = np.stack(split_table(np.kron(eye, table)))
    return stacked, rows, cols


def halves(x):
    high = x.astype(BF16)
    return high, (x - high.astype(F32)).astype(BF16)


def dot(a, b):
    return jnp.dot(a, b, preferred_element_type=F32)


def dot_nt(a, b):
    return lax.dot_general(a, b, (((1,), (1,)), ((), ())), preferred_element_type=F32)


def square_kernel(grad_hbm, out_ref, grad, sems):
    pieces = grad.shape[0]
    rows = grad.shape[1]
    copies = [
        pltpu.make_async_copy(grad_hbm.at[pl.ds(n * rows, rows)], grad.at[n], sems.at[n]) for n in range(pieces)
    ]
    for copy in copies:
        copy.start()
    part = jnp.zeros((8, LANES), F32)
    for n, copy in enumerate(copies):
        copy.wait()
        g = grad[n].astype(F32)
        g = g * g
        g = g.reshape(-1, 8, g.shape[1]).sum(axis=0)
        part += sum(g[:, n * LANES:(n + 1) * LANES] for n in range(g.shape[1] // LANES))
    for n in range(out_ref.shape[0]):
        out_ref[n] = part


def table_rows(freqs, stacked):
    places, wide = [], freqs.shape[0] * LANES
    for n in (0, 1):
        index = lax.shift_right_logical(freqs, 6) if n == 0 else lax.bitwise_and(freqs, GROUP - 1)
        places += [index[s:s + 1, :] for s in range(freqs.shape[0])]
    row = lax.broadcasted_iota(jnp.int32, (GROUP, 2 * wide), 0)
    hot = jnp.where(row == jnp.concatenate(places, axis=1), 1.0, 0.0).astype(BF16)
    return dot(stacked, hot).astype(BF16)


def parts(table, s):
    a = slice(s * LANES, (s + 1) * LANES)
    b = slice((s + 8) * LANES, (s + 9) * LANES)
    return table[:GROUP, a], table[GROUP:, a], table[:GROUP, b], table[GROUP:, b]


def diagonal(x):
    lane = lax.broadcasted_iota(jnp.int32, x.shape, 1)
    zero = jnp.zeros_like(x)
    return jnp.concatenate([jnp.where(lane // TOPK == m, x, zero) for m in range(4)], axis=0)


def tile_of(step):
    return pl.ds(pl.multiple_of(step % 2 * TILE[0], TILE[0]), TILE[0]), pl.ds(pl.multiple_of(step // 2 * TILE[1], TILE[1]), TILE[1])


def fetch(mom_hbm, grad_hbm, mom, grad, sems):
    return [
        (
            pltpu.make_async_copy(mom_hbm.at[tile_of(n)], mom.at[n], sems.at[0, n]),
            pltpu.make_async_copy(grad_hbm.at[tile_of(n)], grad.at[n], sems.at[1, n]),
        )
        for n in range(4)
    ]


def arrive(step, mom_hbm, grad_hbm, mom, grad, sems):
    pltpu.make_async_copy(mom_hbm.at[tile_of(step)], mom.at[step], sems.at[0, step]).wait()
    pltpu.make_async_copy(grad_hbm.at[tile_of(step)], grad.at[step], sems.at[1, step]).wait()


def kept_kernel(flag_ref, mom_hbm, grad_hbm, freq_hbm, stacked_hbm, out_ref, mom, grad, sems, freq_ref, stacked_ref, small_sems, freq_rows, table):
    first = [
        pltpu.make_async_copy(freq_hbm, freq_ref, small_sems.at[0]),
        pltpu.make_async_copy(stacked_hbm, stacked_ref, small_sems.at[1]),
    ]
    for copy in first:
        copy.start()
    for pair in fetch(mom_hbm, grad_hbm, mom, grad, sems):
        for copy in pair:
            copy.start()
    for copy in first:
        copy.wait()
    for col in range(2):
        freq_rows[16 * col:16 * col + 16, :] = jnp.concatenate([freq_ref[:, 4 * col + m, :] for m in range(4)], axis=1)

    flag = (flag_ref[0] == 1).astype(F32)
    stacked = stacked_ref[...]
    chunks = freq_rows.shape[0]
    table[0] = table_rows(freq_rows[:8, :], stacked)

    def one(step, carry):
        at = pl.multiple_of(step * 8, 8)
        later = jnp.minimum(step + 1, 3)
        arrive(step, mom_hbm, grad_hbm, mom, grad, sems)
        freqs = freq_rows[pl.ds(at, 8), :]
        us, vs = [], []
        for s in range(8):
            rows = slice(s * GROUP, (s + 1) * GROUP)
            ah, al, bh, bl = parts(table.at[step % 2], s)
            weights = jnp.concatenate([diagonal(bh), diagonal(bl)], axis=1)
            xh, xl = halves(mom[step, rows, :])
            y = dot(jnp.concatenate([xh, xl, grad[step, rows, :]], axis=0), weights)
            y = y[:, :LANES] + y[:, LANES:]
            a = ah.astype(F32) + al.astype(F32)
            km = jnp.sum((y[:GROUP] + y[GROUP:2 * GROUP]) * a, axis=0, keepdims=True)
            kg = jnp.sum(y[2 * GROUP:] * a, axis=0, keepdims=True)
            us.append(DECAY * km + (1.0 - flag) * kg)
            vs.append(flag * kg)
        table[(step + 1) % 2] = table_rows(freq_rows[pl.ds(pl.multiple_of(later * 8, 8), 8), :], stacked)
        out_ref[pl.ds(at, 8), :] = jnp.concatenate(us, axis=0)
        out_ref[pl.ds(chunks + at, 8), :] = jnp.concatenate(vs, axis=0)
        out_ref[pl.ds(2 * chunks + at, 8), :] = freqs.astype(F32)
        return carry

    lax.fori_loop(0, 4, one, 0)


def message_kernel(kept_ref, square_ref, out_hbm, message, sems):
    rows = kept_ref.shape[0]
    message[:rows, :] = kept_ref[...]
    message[rows:, :] = jnp.sum(square_ref[...], axis=0)
    copies = [pltpu.make_async_copy(message, out_hbm.at[n], sems.at[n]) for n in range(out_hbm.shape[0])]
    for copy in copies:
        copy.start()
    for copy in copies:
        copy.wait()


def own_kernel(flag_ref, mom_hbm, grad_hbm, kept_ref, stacked_ref, u_ref, v_ref, mom, grad, sems):
    step = pl.program_id(0)

    @pl.when(step == 0)
    def _():
        for pair in fetch(mom_hbm, grad_hbm, mom, grad, sems):
            for copy in pair:
                copy.start()

    arrive(step, mom_hbm, grad_hbm, mom, grad, sems)
    flag = (flag_ref[0] == 1).astype(F32)
    stacked = stacked_ref[...]
    chunks = kept_ref.shape[0] // 3
    at = pl.multiple_of(step * 8, 8)
    us = kept_ref[pl.ds(at, 8), :]
    vs = kept_ref[pl.ds(chunks + at, 8), :]
    table = table_rows(kept_ref[pl.ds(2 * chunks + at, 8), :].astype(jnp.int32), stacked)
    for s in range(8):
        rows = slice(s * GROUP, (s + 1) * GROUP)
        ah, al, bh, bl = parts(table, s)
        a = ah.astype(F32) + al.astype(F32)
        high, low = halves(jnp.concatenate([a * us[s:s + 1, :], a * vs[s:s + 1, :]], axis=0))
        left = jnp.concatenate([high, low], axis=0)
        right = jnp.concatenate([high, jnp.zeros_like(low)], axis=0)
        y = dot_nt(jnp.concatenate([left, right], axis=1), jnp.concatenate([diagonal(bh), diagonal(bl)], axis=1))
        g = grad[step, rows, :].astype(F32)
        u_ref[rows, :] = DECAY * mom[step, rows, :] + (1.0 - flag) * g - (y[:GROUP] + y[2 * GROUP:3 * GROUP])
        v_ref[rows, :] = flag * g - (y[GROUP:2 * GROUP] + y[3 * GROUP:])


def update_kernel(count, all_ref, u_ref, v_ref, rows_ref, cols_ref, mom_out, update_out, lists_a, lists_b, lists_h, lists_l, pooled,
                  factor_ref):
    step = pl.program_id(0)
    replicas = all_ref.shape[0]
    chunks = (all_ref.shape[1] - 8) // 3

    @pl.when(step == 0)
    def _():
        total = jnp.sum(all_ref[:, 3 * chunks:, :], axis=0)
        total = jnp.sum(total, axis=(0, 1), keepdims=True)
        rms = jnp.sqrt(total * (1.0 / count))
        factor_ref[...] = jnp.broadcast_to(jnp.minimum(jnp.float32(1.0), CLIP_RMS / (rms + 1e-06)), factor_ref.shape)

    factor = factor_ref[...]
    lane = lax.broadcasted_iota(jnp.int32, (8, LANES), 1) // TOPK

    def regroup(xs, m):
        moved = [x if r == m else pltpu.roll(x, (TOPK * (r - m)) % LANES, 1) for r, x in enumerate(xs)]
        out = moved[0]
        for r in range(1, 4):
            out = jnp.where(lane == r, moved[r], out)
        return out

    def prepare(tile, slot):
        at = pl.multiple_of(tile * 8, 8)
        for group in range(replicas // 4):
            ks, fs = [], []
            for r in range(4 * group, 4 * group + 4):
                u = all_ref[r, pl.ds(at, 8), :]
                v = all_ref[r, pl.ds(chunks + at, 8), :]
                ks.append((u + factor * v) * (1.0 / replicas))
                fs.append(all_ref[r, pl.ds(2 * chunks + at, 8), :])
            for m in range(4):
                k = regroup(ks, m)
                f = regroup(fs, m).astype(jnp.int32)
                high = k.astype(BF16).astype(F32)
                place = slice(group * LANES, (group + 1) * LANES)
                lists_a[slot, m, :, place] = lax.shift_right_logical(f, 6)
                lists_b[slot, m, :, place] = lax.bitwise_and(f, GROUP - 1)
                lists_h[slot, m, :, place] = high
                lists_l[slot, m, :, place] = k - high

    items = replicas * TOPK
    place = lax.broadcasted_iota(jnp.int32, (GROUP, items), 0)

    def scatter(s, m, slot):
        here = slice(s, s + 1)
        hit = place == lists_a[slot, m, here, :]
        high = jnp.where(hit, lists_h[slot, m, here, :], 0.0).astype(BF16)
        low = jnp.where(hit, lists_l[slot, m, here, :], 0.0).astype(BF16)
        hot = jnp.where(place == lists_b[slot, m, here, :], 1.0, 0.0).astype(BF16)
        out = dot_nt(jnp.concatenate([high, low], axis=0), hot)
        return out[:GROUP] + out[GROUP:]

    def scatter_rows(first, last, slot):
        for s in range(first, last):
            for pair in range(2):
                both = jnp.concatenate([scatter(s, 2 * pair, slot), scatter(s, 2 * pair + 1, slot)], axis=1)
                pooled[slot, s * GROUP:(s + 1) * GROUP, pair * LANES:(pair + 1) * LANES] = both

    def columns(slot):
        ph, plow = halves(pooled[slot])
        ch, cl = cols_ref[0], cols_ref[1]
        return dot(ph, ch) + dot(plow, ch) + dot(ph, cl)

    def finish(y):
        rh, rl = rows_ref[0], rows_ref[1]
        for half in range(2):
            part = slice(half * 256, (half + 1) * 256)
            yh, yl = halves(y[part, :])
            update_out[part, :] = dot(rh, yh) + dot(rh, yl) + dot(rl, yh)

    def new_momentum():
        mom_out[...] = u_ref[...] + factor[:1, :1] * v_ref[...]

    @pl.when(step == 0)
    def _():
        prepare(0, 0)
        scatter_rows(0, 8, 0)
        new_momentum()
        prepare(1, 1)

    @pl.when(jnp.logical_and(step > 0, step < 4))
    def _():
        slot = step % 2
        y = columns(1 - slot)
        scatter_rows(0, 4, slot)
        finish(y)
        scatter_rows(4, 8, slot)
        new_momentum()
        prepare(jnp.minimum(step + 1, 3), 1 - slot)

    @pl.when(step == 4)
    def _():
        finish(columns(1))


def full(shape):
    return pl.BlockSpec(shape, lambda i: (0,) * len(shape))


def body(momentum, gradient, kept_freq, clip_flag):
    replicas, tensors = lax.axis_size("replica"), lax.axis_size("tensor")
    mom, grad, freq = momentum[0], gradient[0], kept_freq[0]
    rows, cols = mom.shape
    steps = 4
    chunks = rows // GROUP * cols // GROUP * TOPK // LANES
    stacked, row_table, col_table = (jnp.asarray(t) for t in tables())
    tile = pl.BlockSpec(TILE, lambda i: (i % 2, i // 2))
    scalar = pl.BlockSpec(memory_space=pltpu.SMEM)
    hbm = pl.BlockSpec(memory_space=pltpu.HBM)
    limit = pltpu.CompilerParams(vmem_limit_bytes=60 * 1024 * 1024)
    small = pltpu.CompilerParams(vmem_limit_bytes=32 * 1024 * 1024)
    landing = [pltpu.VMEM((steps,) + TILE, F32), pltpu.VMEM((steps,) + TILE, BF16), pltpu.SemaphoreType.DMA((2, steps))]

    squares = pl.pallas_call(
        square_kernel,
        in_specs=[hbm],
        out_specs=pl.BlockSpec(memory_space=pltpu.VMEM),
        out_shape=jax.ShapeDtypeStruct((tensors, 8, LANES), F32),
        scratch_shapes=[pltpu.VMEM((4, rows // 4, cols), BF16), pltpu.SemaphoreType.DMA((4,))],
        compiler_params=limit,
    )(grad)
    squares = lax.all_to_all(squares, "tensor", 0, 0)

    kept = pl.pallas_call(
        kept_kernel,
        in_specs=[scalar, hbm, hbm, hbm, hbm],
        out_specs=pl.BlockSpec(memory_space=pltpu.VMEM),
        out_shape=jax.ShapeDtypeStruct((3 * chunks, LANES), F32),
        scratch_shapes=landing
        + [
            pltpu.VMEM(freq.shape, jnp.int32),
            pltpu.VMEM(stacked.shape, BF16),
            pltpu.SemaphoreType.DMA((2,)),
            pltpu.VMEM((chunks, LANES), jnp.int32),
            pltpu.VMEM((2, 2 * GROUP, 16 * LANES), BF16),
        ],
        compiler_params=limit,
        cost_estimate=pl.CostEstimate(flops=2 * 10 ** 9, bytes_accessed=3 * 2 ** 20, transcendentals=0),
    )(clip_flag, mom, grad, freq, stacked)

    message = pl.pallas_call(
        message_kernel,
        in_specs=[pl.BlockSpec(memory_space=pltpu.VMEM)] * 2,
        out_specs=hbm,
        out_shape=jax.ShapeDtypeStruct((replicas, 3 * chunks + 8, LANES), F32),
        scratch_shapes=[pltpu.VMEM((3 * chunks + 8, LANES), F32), pltpu.SemaphoreType.DMA((replicas,))],
        compiler_params=small,
    )(kept, squares)
    everyone = lax.all_to_all(message, "replica", 0, 0)

    own_u, own_v = pl.pallas_call(
        own_kernel,
        grid=(steps,),
        in_specs=[scalar, hbm, hbm, full(kept.shape), full(stacked.shape)],
        out_specs=[tile, tile],
        out_shape=[jax.ShapeDtypeStruct((rows, cols), F32)] * 2,
        scratch_shapes=landing,
        compiler_params=limit,
        cost_estimate=pl.CostEstimate(flops=2 * 10 ** 9, bytes_accessed=7 * 2 ** 20, transcendentals=0),
    )(clip_flag, mom, grad, kept, stacked)

    early = pl.BlockSpec(TILE, lambda i: (jnp.minimum(i, 3) % 2, jnp.minimum(i, 3) // 2))
    late = pl.BlockSpec(TILE, lambda i: (jnp.maximum(i - 1, 0) % 2, jnp.maximum(i - 1, 0) // 2))
    new_mom, update = pl.pallas_call(
        lambda *refs: update_kernel(replicas * tensors * rows * cols, *refs),
        grid=(steps + 1,),
        in_specs=[full(everyone.shape), early, early, full(row_table.shape), full(col_table.shape)],
        out_specs=[early, late],
        out_shape=[jax.ShapeDtypeStruct((rows, cols), F32)] * 2,
        scratch_shapes=[pltpu.VMEM((2, 4, 8, replicas * TOPK), t) for t in (jnp.int32, jnp.int32, F32, F32)]
        + [pltpu.VMEM((2,) + TILE, F32), pltpu.VMEM((8, LANES), F32)],
        compiler_params=pltpu.CompilerParams(vmem_limit_bytes=58 * 1024 * 1024),
    )(everyone, own_u, own_v, row_table, col_table)
    return (new_mom[None], update)


def solution(mesh):
    placed = (
        P("replica", None, "tensor"),
        P("replica", None, "tensor"),
        P("replica", None, "tensor", None),
        P("replica"),
    )
    return jax.shard_map(
        body,
        mesh=mesh,
        in_specs=placed,
        out_specs=(P("replica", None, "tensor"), P(None, "tensor")),
        check_vma=False,
    )
```

```python
import math

import jax
import jax.numpy as jnp
import ml_dtypes
import numpy as np
from jax import lax
from jax.experimental import pallas as pl
from jax.experimental.pallas import tpu as pltpu
from jax.sharding import PartitionSpec as P

GROUP = 64
TOPK = 32
LANES = 128
TILE = (512, 256)
CLIP_RMS = 0.5
DECAY = 0.9
F32 = jnp.float32
BF16 = jnp.bfloat16


def split_table(table):
    high = table.astype(ml_dtypes.bfloat16)
    low = (table - high.astype(np.float64)).astype(ml_dtypes.bfloat16)
    return high, low


def tables():
    freq = np.arange(GROUP)[:, None]
    place = np.arange(GROUP)[None, :]
    table = np.sqrt(np.where(freq == 0, 1.0, 2.0) / GROUP) * np.cos(math.pi * (2 * place + 1) * freq / (2 * GROUP))
    high, low = split_table(table)
    stacked = np.concatenate([high.T, low.T], axis=0)
    eye = np.eye(4)
    rows = np.stack(split_table(np.kron(eye, table.T)))
    cols = np.stack(split_table(np.kron(eye, table)))
    return stacked, rows, cols


def halves(x):
    high = x.astype(BF16)
    return high, (x - high.astype(F32)).astype(BF16)


def dot(a, b):
    return jnp.dot(a, b, preferred_element_type=F32)


def dot_nt(a, b):
    return lax.dot_general(a, b, (((1,), (1,)), ((), ())), preferred_element_type=F32)


def square_kernel(grad_hbm, mom_hbm, freq_hbm, square_hbm, grad_ref, mom_ref, freq_rows, freq_ref, squares, sems, grad_sems):
    pieces = 4
    rows = grad_ref.shape[0] // pieces
    small = pltpu.make_async_copy(freq_hbm, freq_ref, sems.at[0])
    large = []
    for n in range(pieces):
        here = pl.ds(n * rows, rows)
        large.append(pltpu.make_async_copy(grad_hbm.at[here], grad_ref.at[here], grad_sems.at[n]))
    rest = pltpu.make_async_copy(mom_hbm, mom_ref, sems.at[1])
    for copy in large + [small, rest]:
        copy.start()
    part = jnp.zeros((8, LANES), F32)
    for n, copy in enumerate(large):
        copy.wait()
        g = grad_ref[n * rows:(n + 1) * rows, :].astype(F32)
        g = g * g
        g = g.reshape(-1, 8, g.shape[1]).sum(axis=0)
        part += sum(g[:, m * LANES:(m + 1) * LANES] for m in range(g.shape[1] // LANES))
    for n in range(squares.shape[0]):
        squares[n] = part
    result = pltpu.make_async_copy(squares, square_hbm, sems.at[2])
    result.start()
    small.wait()
    for col in range(2):
        freq_rows[16 * col:16 * col + 16, :] = jnp.concatenate([freq_ref[:, 4 * col + m, :] for m in range(4)], axis=1)
    rest.wait()
    result.wait()


def table_rows(freqs, stacked):
    places, wide = [], freqs.shape[0] * LANES
    for n in (0, 1):
        index = lax.shift_right_logical(freqs, 6) if n == 0 else lax.bitwise_and(freqs, GROUP - 1)
        places += [index[s:s + 1, :] for s in range(freqs.shape[0])]
    row = lax.broadcasted_iota(jnp.int32, (GROUP, 2 * wide), 0)
    hot = jnp.where(row == jnp.concatenate(places, axis=1), 1.0, 0.0).astype(BF16)
    return dot(stacked, hot).astype(BF16)


def parts(table, s):
    a = slice(s * LANES, (s + 1) * LANES)
    b = slice((s + 8) * LANES, (s + 9) * LANES)
    return table[:GROUP, a], table[GROUP:, a], table[:GROUP, b], table[GROUP:, b]


def diagonal(x):
    lane = lax.broadcasted_iota(jnp.int32, x.shape, 1)
    zero = jnp.zeros_like(x)
    return jnp.concatenate([jnp.where(lane // TOPK == m, x, zero) for m in range(4)], axis=0)


def tile_of(step):
    return pl.multiple_of(step % 2 * TILE[0], TILE[0]), pl.ds(pl.multiple_of(step // 2 * TILE[1], TILE[1]), TILE[1])


def kept_kernel(flag_ref, mom_ref, grad_ref, freq_rows, stacked_ref, out_ref, table):
    flag = (flag_ref[0] == 1).astype(F32)
    stacked = stacked_ref[...]
    chunks = freq_rows.shape[0]
    table[0] = table_rows(freq_rows[:8, :], stacked)

    def one(step, carry):
        at = pl.multiple_of(step * 8, 8)
        later = pl.multiple_of(jnp.minimum(step + 1, 3) * 8, 8)
        top, cols = tile_of(step)
        freqs = freq_rows[pl.ds(at, 8), :]
        us, vs = [], []
        for s in range(8):
            rows = pl.ds(top + s * GROUP, GROUP)
            ah, al, bh, bl = parts(table.at[step % 2], s)
            weights = jnp.concatenate([diagonal(bh), diagonal(bl)], axis=1)
            xh, xl = halves(mom_ref[rows, cols])
            y = dot(jnp.concatenate([xh, xl, grad_ref[rows, cols]], axis=0), weights)
            y = y[:, :LANES] + y[:, LANES:]
            a = ah.astype(F32) + al.astype(F32)
            km = jnp.sum((y[:GROUP] + y[GROUP:2 * GROUP]) * a, axis=0, keepdims=True)
            kg = jnp.sum(y[2 * GROUP:] * a, axis=0, keepdims=True)
            us.append(DECAY * km + (1.0 - flag) * kg)
            vs.append(flag * kg)
        table[(step + 1) % 2] = table_rows(freq_rows[pl.ds(later, 8), :], stacked)
        out_ref[pl.ds(at, 8), :] = jnp.concatenate(us, axis=0)
        out_ref[pl.ds(chunks + at, 8), :] = jnp.concatenate(vs, axis=0)
        out_ref[pl.ds(2 * chunks + at, 8), :] = freqs.astype(F32)
        return carry

    lax.fori_loop(0, 4, one, 0)


def message_kernel(kept_ref, square_ref, out_hbm, message, sems):
    rows = kept_ref.shape[0]
    message[:rows, :] = kept_ref[...]
    message[rows:, :] = jnp.sum(square_ref[...], axis=0)
    copies = [pltpu.make_async_copy(message, out_hbm.at[n], sems.at[n]) for n in range(out_hbm.shape[0])]
    for copy in copies:
        copy.start()
    for copy in copies:
        copy.wait()


def tile_copies(step, pairs, sems):
    top, cols = tile_of(step)
    out = []
    for n, (hbm, tiles, outward) in enumerate(pairs):
        far, near = hbm.at[pl.ds(top, TILE[0]), cols], tiles.at[step]
        out.append(pltpu.make_async_copy(near if outward else far, far if outward else near, sems.at[n, step]))
    return out


def own_kernel(flag_ref, mom_hbm, grad_hbm, kept_ref, stacked_ref, u_hbm, v_hbm, mom, grad, u_out, v_out, in_sems, out_sems):
    inward = [(mom_hbm, mom, False), (grad_hbm, grad, False)]
    outward = [(u_hbm, u_out, True), (v_hbm, v_out, True)]
    for step in range(4):
        for copy in tile_copies(step, inward, in_sems):
            copy.start()
    flag = (flag_ref[0] == 1).astype(F32)
    stacked = stacked_ref[...]
    chunks = kept_ref.shape[0] // 3

    def one(step, carry):
        at = pl.multiple_of(step * 8, 8)
        us = kept_ref[pl.ds(at, 8), :]
        vs = kept_ref[pl.ds(chunks + at, 8), :]
        table = table_rows(kept_ref[pl.ds(2 * chunks + at, 8), :].astype(jnp.int32), stacked)
        for copy in tile_copies(step, inward, in_sems):
            copy.wait()
        for s in range(8):
            rows = slice(s * GROUP, (s + 1) * GROUP)
            ah, al, bh, bl = parts(table, s)
            a = ah.astype(F32) + al.astype(F32)
            high, low = halves(jnp.concatenate([a * us[s:s + 1, :], a * vs[s:s + 1, :]], axis=0))
            left = jnp.concatenate([high, low], axis=0)
            right = jnp.concatenate([high, jnp.zeros_like(low)], axis=0)
            y = dot_nt(jnp.concatenate([left, right], axis=1), jnp.concatenate([diagonal(bh), diagonal(bl)], axis=1))
            g = grad[step, rows, :].astype(F32)
            u_out[step, rows, :] = DECAY * mom[step, rows, :] + (1.0 - flag) * g - (y[:GROUP] + y[2 * GROUP:3 * GROUP])
            v_out[step, rows, :] = flag * g - (y[GROUP:2 * GROUP] + y[3 * GROUP:])
        for copy in tile_copies(step, outward, out_sems):
            copy.start()
        return carry

    lax.fori_loop(0, 4, one, 0)
    for step in range(4):
        for copy in tile_copies(step, outward, out_sems):
            copy.wait()


def update_kernel(count, all_ref, u_hbm, v_hbm, rows_ref, cols_ref, mom_hbm, update_hbm, lists_a, lists_b, lists_h, lists_l, pooled,
                  u_ref, v_ref, mom_out, update_out, in_sems, mom_sems, update_sems):
    inward = [(u_hbm, u_ref, False), (v_hbm, v_ref, False)]
    for tile in range(4):
        for copy in tile_copies(tile, inward, in_sems):
            copy.start()
    replicas = all_ref.shape[0]
    chunks = (all_ref.shape[1] - 8) // 3
    total = jnp.sum(all_ref[:, 3 * chunks:, :], axis=0)
    total = jnp.sum(total, axis=(0, 1), keepdims=True)
    rms = jnp.sqrt(total * (1.0 / count))
    factor = jnp.minimum(jnp.float32(1.0), CLIP_RMS / (rms + 1e-06))
    lane = lax.broadcasted_iota(jnp.int32, (8, LANES), 1) // TOPK
    half = TILE[0] // 2

    def regroup(xs, m):
        moved = [x if r == m else pltpu.roll(x, (TOPK * (r - m)) % LANES, 1) for r, x in enumerate(xs)]
        out = moved[0]
        for r in range(1, 4):
            out = jnp.where(lane == r, moved[r], out)
        return out

    def prepare(tile, slot):
        at = pl.multiple_of(tile * 8, 8)
        for group in range(replicas // 4):
            ks, fs = [], []
            for r in range(4 * group, 4 * group + 4):
                u = all_ref[r, pl.ds(at, 8), :]
                v = all_ref[r, pl.ds(chunks + at, 8), :]
                ks.append((u + factor * v) * (1.0 / replicas))
                fs.append(all_ref[r, pl.ds(2 * chunks + at, 8), :])
            for m in range(4):
                k = regroup(ks, m)
                f = regroup(fs, m).astype(jnp.int32)
                high = k.astype(BF16).astype(F32)
                place = slice(group * LANES, (group + 1) * LANES)
                lists_a[slot, m, :, place] = lax.shift_right_logical(f, 6)
                lists_b[slot, m, :, place] = lax.bitwise_and(f, GROUP - 1)
                lists_h[slot, m, :, place] = high
                lists_l[slot, m, :, place] = k - high

    items = replicas * TOPK
    place = lax.broadcasted_iota(jnp.int32, (GROUP, items), 0)

    def scatter(s, m, slot):
        here = slice(s, s + 1)
        hit = place == lists_a[slot, m, here, :]
        high = jnp.where(hit, lists_h[slot, m, here, :], 0.0).astype(BF16)
        low = jnp.where(hit, lists_l[slot, m, here, :], 0.0).astype(BF16)
        hot = jnp.where(place == lists_b[slot, m, here, :], 1.0, 0.0).astype(BF16)
        out = dot_nt(jnp.concatenate([high, low], axis=0), hot)
        return out[:GROUP] + out[GROUP:]

    def scatter_rows(part, slot):
        for s in range(4):
            for pair in range(2):
                both = [scatter(4 * part + s, 2 * pair + n, slot) for n in range(2)]
                pooled[part, s * GROUP:(s + 1) * GROUP, pair * LANES:(pair + 1) * LANES] = jnp.concatenate(both, axis=1)

    def inverse(tile, part):
        ph, plow = halves(pooled[part])
        ch, cl = cols_ref[0], cols_ref[1]
        yh, yl = halves(dot(ph, ch) + dot(plow, ch) + dot(ph, cl))
        rh, rl = rows_ref[0], rows_ref[1]
        update_out[tile, part] = dot(rh, yh) + dot(rh, yl) + dot(rl, yh)

    def update_copy(tile, part):
        top, cols = tile_of(tile)
        there = update_hbm.at[pl.ds(top + part * half, half), cols]
        return pltpu.make_async_copy(update_out.at[tile, part], there, update_sems.at[tile, part])

    def mom_copy(tile):
        return tile_copies(tile, [(mom_hbm, mom_out, True)], mom_sems)[0]

    pooled[1] = jnp.zeros(pooled.shape[1:], F32)
    prepare(0, 0)

    def one(tile, carry):
        slot = tile % 2
        before = jnp.maximum(tile - 1, 0)
        scatter_rows(0, slot)
        inverse(before, 1)
        scatter_rows(1, slot)
        inverse(tile, 0)
        for copy in tile_copies(tile, inward, in_sems):
            copy.wait()
        mom_out[tile] = u_ref[tile] + factor * v_ref[tile]
        prepare(jnp.minimum(tile + 1, 3), 1 - slot)
        mom_copy(tile).start()
        update_copy(tile, 0).start()

        @pl.when(tile > 0)
        def _():
            update_copy(before, 1).start()

        return carry

    lax.fori_loop(0, 4, one, 0)
    inverse(3, 1)
    update_copy(3, 1).start()
    for tile in range(4):
        mom_copy(tile).wait()
        for part in range(2):
            update_copy(tile, part).wait()


def body(momentum, gradient, kept_freq, clip_flag):
    replicas, tensors = lax.axis_size("replica"), lax.axis_size("tensor")
    mom, grad, freq = momentum[0], gradient[0], kept_freq[0]
    rows, cols = mom.shape
    chunks = rows // GROUP * cols // GROUP * TOPK // LANES
    stacked, row_table, col_table = (jnp.asarray(t) for t in tables())
    scalar = pl.BlockSpec(memory_space=pltpu.SMEM)
    hbm = pl.BlockSpec(memory_space=pltpu.HBM)
    vmem = pl.BlockSpec(memory_space=pltpu.VMEM)
    limit = pltpu.CompilerParams(vmem_limit_bytes=32 * 1024 * 1024)
    far = lambda x: pltpu.with_memory_space_constraint(x, pltpu.HBM)
    near = lambda x: pltpu.with_memory_space_constraint(x, pltpu.VMEM)

    squares, grad_near, mom_near, freq_rows = pl.pallas_call(
        square_kernel,
        in_specs=[hbm] * 3,
        out_specs=[hbm] + [vmem] * 3,
        out_shape=[
            pltpu.HBM((tensors, 8, LANES), F32),
            pltpu.VMEM(grad.shape, BF16),
            pltpu.VMEM(mom.shape, F32),
            pltpu.VMEM((chunks, LANES), jnp.int32),
        ],
        scratch_shapes=[
            pltpu.VMEM(freq.shape, jnp.int32),
            pltpu.VMEM((tensors, 8, LANES), F32),
            pltpu.SemaphoreType.DMA((3,)),
            pltpu.SemaphoreType.DMA((4,)),
        ],
        compiler_params=limit,
    )(far(grad), far(mom), far(freq))
    squares = lax.all_to_all(squares, "tensor", 0, 0)

    kept = pl.pallas_call(
        kept_kernel,
        in_specs=[scalar] + [vmem] * 4,
        out_specs=vmem,
        out_shape=pltpu.VMEM((3 * chunks, LANES), F32),
        scratch_shapes=[pltpu.VMEM((2, 2 * GROUP, 16 * LANES), BF16)],
        compiler_params=limit,
        cost_estimate=pl.CostEstimate(flops=2 * 10 ** 9, bytes_accessed=3 * 2 ** 20, transcendentals=0),
    )(clip_flag, near(mom_near), near(grad_near), near(freq_rows), near(stacked))

    message = pl.pallas_call(
        message_kernel,
        in_specs=[vmem] * 2,
        out_specs=hbm,
        out_shape=pltpu.HBM((replicas, 3 * chunks + 8, LANES), F32),
        scratch_shapes=[pltpu.VMEM((3 * chunks + 8, LANES), F32), pltpu.SemaphoreType.DMA((replicas,))],
        compiler_params=limit,
    )(near(kept), near(squares))
    everyone = lax.all_to_all(message, "replica", 0, 0)

    own_u, own_v = pl.pallas_call(
        own_kernel,
        in_specs=[scalar, hbm, hbm, vmem, vmem],
        out_specs=[hbm] * 2,
        out_shape=[pltpu.HBM((rows, cols), F32)] * 2,
        scratch_shapes=[pltpu.VMEM((4,) + TILE, t) for t in (F32, BF16, F32, F32)] + [pltpu.SemaphoreType.DMA((2, 4))] * 2,
        compiler_params=limit,
        cost_estimate=pl.CostEstimate(flops=2 * 10 ** 9, bytes_accessed=7 * 2 ** 20, transcendentals=0),
    )(clip_flag, far(mom), far(grad), near(kept), near(stacked))

    new_mom, update = pl.pallas_call(
        lambda *refs: update_kernel(replicas * tensors * rows * cols, *refs),
        in_specs=[vmem, hbm, hbm, vmem, vmem],
        out_specs=[hbm] * 2,
        out_shape=[jax.ShapeDtypeStruct((rows, cols), F32)] * 2,
        scratch_shapes=[pltpu.VMEM((2, 4, 8, replicas * TOPK), t) for t in (jnp.int32, jnp.int32, F32, F32)]
        + [
            pltpu.VMEM((2, TILE[0] // 2, TILE[1]), F32),
            pltpu.VMEM((4,) + TILE, F32),
            pltpu.VMEM((4,) + TILE, F32),
            pltpu.VMEM((4,) + TILE, F32),
            pltpu.VMEM((4, 2, TILE[0] // 2, TILE[1]), F32),
            pltpu.SemaphoreType.DMA((2, 4)),
            pltpu.SemaphoreType.DMA((1, 4)),
            pltpu.SemaphoreType.DMA((4, 2)),
        ],
        compiler_params=limit,
    )(near(everyone), far(own_u), far(own_v), near(row_table), near(col_table))
    return (new_mom[None], update)


def solution(mesh):
    placed = (
        P("replica", None, "tensor"),
        P("replica", None, "tensor"),
        P("replica", None, "tensor", None),
        P("replica"),
    )
    return jax.shard_map(
        body,
        mesh=mesh,
        in_specs=placed,
        out_specs=(P("replica", None, "tensor"), P(None, "tensor")),
        check_vma=False,
    )
```

```python
import math

import jax
import jax.numpy as jnp
import ml_dtypes
import numpy as np
from jax import lax
from jax.experimental import pallas as pl
from jax.experimental.pallas import tpu as pltpu
from jax.sharding import PartitionSpec as P

GROUP = 64
TOPK = 32
LANES = 128
TILE = (512, 256)
CLIP_RMS = 0.5
DECAY = 0.9
F32 = jnp.float32
BF16 = jnp.bfloat16


def split_table(table):
    high = table.astype(ml_dtypes.bfloat16)
    low = (table - high.astype(np.float64)).astype(ml_dtypes.bfloat16)
    return high, low


def tables():
    freq = np.arange(GROUP)[:, None]
    place = np.arange(GROUP)[None, :]
    table = np.sqrt(np.where(freq == 0, 1.0, 2.0) / GROUP) * np.cos(math.pi * (2 * place + 1) * freq / (2 * GROUP))
    high, low = split_table(table)
    stacked = np.concatenate([high.T, low.T], axis=0)
    pair = [np.kron(np.eye(2), t.astype(np.float64)) for t in (high, low)]
    none = np.zeros_like(pair[0])
    cols = np.block([[pair[0], pair[1]], [pair[0], none]]).astype(ml_dtypes.bfloat16)
    rows = np.block([[pair[0].T, pair[0].T], [pair[1].T, none]]).astype(ml_dtypes.bfloat16)
    return stacked, rows, cols


def halves(x):
    high = x.astype(BF16)
    return high, (x - high.astype(F32)).astype(BF16)


def dot(a, b):
    return jnp.dot(a, b, preferred_element_type=F32)


def dot_nt(a, b):
    return lax.dot_general(a, b, (((1,), (1,)), ((), ())), preferred_element_type=F32)


def square_kernel(grad_hbm, freq_hbm, square_hbm, grad_ref, freq_rows, freq_ref, squares, sems, grad_sems):
    pieces = 4
    rows = grad_ref.shape[0] // pieces
    small = pltpu.make_async_copy(freq_hbm, freq_ref, sems.at[0])
    large = []
    for n in range(pieces):
        here = pl.ds(n * rows, rows)
        large.append(pltpu.make_async_copy(grad_hbm.at[here], grad_ref.at[here], grad_sems.at[n]))
    for copy in large + [small]:
        copy.start()
    part = jnp.zeros((8, LANES), F32)
    for n, copy in enumerate(large):
        copy.wait()
        g = grad_ref[n * rows:(n + 1) * rows, :].astype(F32)
        g = g * g
        g = g.reshape(-1, 8, g.shape[1]).sum(axis=0)
        part += sum(g[:, m * LANES:(m + 1) * LANES] for m in range(g.shape[1] // LANES))
    for n in range(squares.shape[0]):
        squares[n] = part
    result = pltpu.make_async_copy(squares, square_hbm, sems.at[1])
    result.start()
    small.wait()
    for col in range(2):
        freq_rows[16 * col:16 * col + 16, :] = jnp.concatenate([freq_ref[:, 4 * col + m, :] for m in range(4)], axis=1)
    result.wait()


def table_rows(freqs, stacked):
    places, wide = [], freqs.shape[0] * LANES
    for n in (0, 1):
        index = lax.shift_right_logical(freqs, 6) if n == 0 else lax.bitwise_and(freqs, GROUP - 1)
        places += [index[s:s + 1, :] for s in range(freqs.shape[0])]
    row = lax.broadcasted_iota(jnp.int32, (GROUP, 2 * wide), 0)
    hot = jnp.where(row == jnp.concatenate(places, axis=1), 1.0, 0.0).astype(BF16)
    return dot(stacked, hot).astype(BF16)


def parts(table, s):
    a = slice(s * LANES, (s + 1) * LANES)
    b = slice((s + 8) * LANES, (s + 9) * LANES)
    return table[:GROUP, a], table[GROUP:, a], table[:GROUP, b], table[GROUP:, b]


def diagonal(x):
    lane = lax.broadcasted_iota(jnp.int32, x.shape, 1)
    zero = jnp.zeros_like(x)
    return jnp.concatenate([jnp.where(lane // TOPK == m, x, zero) for m in range(4)], axis=0)


def tile_of(step):
    return pl.multiple_of(step % 2 * TILE[0], TILE[0]), pl.ds(pl.multiple_of(step // 2 * TILE[1], TILE[1]), TILE[1])


def tile_copies(step, pairs, sems):
    top, cols = tile_of(step)
    out = []
    for n, (hbm, tiles, outward) in enumerate(pairs):
        far, near = hbm.at[pl.ds(top, TILE[0]), cols], tiles.at[step]
        out.append(pltpu.make_async_copy(near if outward else far, far if outward else near, sems.at[n, step]))
    return out


def kept_kernel(flag_ref, mom_hbm, grad_ref, freq_rows, stacked_ref, out_ref, message_hbm, mom, table, in_sems, out_sems):
    inward = [(mom_hbm, mom, False)]
    for step in range(4):
        for copy in tile_copies(step, inward, in_sems):
            copy.start()
    flag = (flag_ref[0] == 1).astype(F32)
    stacked = stacked_ref[...]
    chunks = freq_rows.shape[0]
    table[0] = table_rows(freq_rows[:8, :], stacked)

    def one(step, carry):
        at = pl.multiple_of(step * 8, 8)
        later = pl.multiple_of(jnp.minimum(step + 1, 3) * 8, 8)
        top, cols = tile_of(step)
        freqs = freq_rows[pl.ds(at, 8), :]
        for copy in tile_copies(step, inward, in_sems):
            copy.wait()
        us, vs = [], []
        for s in range(8):
            rows = slice(s * GROUP, (s + 1) * GROUP)
            ah, al, bh, bl = parts(table.at[step % 2], s)
            weights = jnp.concatenate([diagonal(bh), diagonal(bl)], axis=1)
            xh, xl = halves(mom[step, rows, :])
            y = dot(jnp.concatenate([xh, xl, grad_ref[pl.ds(top + s * GROUP, GROUP), cols]], axis=0), weights)
            y = y[:, :LANES] + y[:, LANES:]
            a = ah.astype(F32) + al.astype(F32)
            km = jnp.sum((y[:GROUP] + y[GROUP:2 * GROUP]) * a, axis=0, keepdims=True)
            kg = jnp.sum(y[2 * GROUP:] * a, axis=0, keepdims=True)
            us.append(DECAY * km + (1.0 - flag) * kg)
            vs.append(flag * kg)
        table[(step + 1) % 2] = table_rows(freq_rows[pl.ds(later, 8), :], stacked)
        out_ref[pl.ds(at, 8), :] = jnp.concatenate(us, axis=0)
        out_ref[pl.ds(chunks + at, 8), :] = jnp.concatenate(vs, axis=0)
        out_ref[pl.ds(2 * chunks + at, 8), :] = freqs.astype(F32)
        return carry

    lax.fori_loop(0, 4, one, 0)
    copies = [
        pltpu.make_async_copy(out_ref, message_hbm.at[n, pl.ds(0, 3 * chunks)], out_sems.at[n])
        for n in range(message_hbm.shape[0])
    ]
    for copy in copies:
        copy.start()
    for copy in copies:
        copy.wait()


def message_kernel(message_hbm, square_ref, out_hbm, total, sems):
    total[...] = jnp.sum(square_ref[...], axis=0)
    replicas, rows = out_hbm.shape[:2]
    copies = [pltpu.make_async_copy(total, out_hbm.at[n, pl.ds(rows - 8, 8)], sems.at[n]) for n in range(replicas)]
    for copy in copies:
        copy.start()
    for copy in copies:
        copy.wait()


def own_kernel(flag_ref, mom_hbm, grad_hbm, kept_ref, stacked_ref, u_hbm, v_hbm, mom, grad, u_out, v_out, in_sems, out_sems):
    inward = [(mom_hbm, mom, False), (grad_hbm, grad, False)]
    outward = [(u_hbm, u_out, True), (v_hbm, v_out, True)]
    for step in range(4):
        for copy in tile_copies(step, inward, in_sems):
            copy.start()
    flag = (flag_ref[0] == 1).astype(F32)
    stacked = stacked_ref[...]
    chunks = kept_ref.shape[0] // 3

    def one(step, carry):
        at = pl.multiple_of(step * 8, 8)
        us = kept_ref[pl.ds(at, 8), :]
        vs = kept_ref[pl.ds(chunks + at, 8), :]
        table = table_rows(kept_ref[pl.ds(2 * chunks + at, 8), :].astype(jnp.int32), stacked)
        for copy in tile_copies(step, inward, in_sems):
            copy.wait()
        for s in range(8):
            rows = slice(s * GROUP, (s + 1) * GROUP)
            ah, al, bh, bl = parts(table, s)
            a = ah.astype(F32) + al.astype(F32)
            high, low = halves(jnp.concatenate([a * us[s:s + 1, :], a * vs[s:s + 1, :]], axis=0))
            left = jnp.concatenate([high, low], axis=0)
            right = jnp.concatenate([high, jnp.zeros_like(low)], axis=0)
            y = dot_nt(jnp.concatenate([left, right], axis=1), jnp.concatenate([diagonal(bh), diagonal(bl)], axis=1))
            g = grad[step, rows, :].astype(F32)
            u_out[step, rows, :] = DECAY * mom[step, rows, :] + (1.0 - flag) * g - (y[:GROUP] + y[2 * GROUP:3 * GROUP])
            v_out[step, rows, :] = flag * g - (y[GROUP:2 * GROUP] + y[3 * GROUP:])
        for copy in tile_copies(step, outward, out_sems):
            copy.start()
        return carry

    lax.fori_loop(0, 4, one, 0)
    for step in range(4):
        for copy in tile_copies(step, outward, out_sems):
            copy.wait()


def update_kernel(count, all_ref, u_hbm, v_hbm, rows_ref, cols_ref, mom_hbm, update_hbm, lists_a, lists_b, lists_h, lists_l, pooled, columns,
                  u_ref, v_ref, mom_out, update_out, in_sems, mom_sems, update_sems):
    inward = [(u_hbm, u_ref, False), (v_hbm, v_ref, False)]
    for tile in range(4):
        for copy in tile_copies(tile, inward, in_sems):
            copy.start()
    replicas = all_ref.shape[0]
    chunks = (all_ref.shape[1] - 8) // 3
    total = jnp.sum(all_ref[:, 3 * chunks:, :], axis=0)
    total = jnp.sum(total, axis=(0, 1), keepdims=True)
    rms = jnp.sqrt(total * (1.0 / count))
    factor = jnp.minimum(jnp.float32(1.0), CLIP_RMS / (rms + 1e-06))
    lane = lax.broadcasted_iota(jnp.int32, (8, LANES), 1) // TOPK
    half = TILE[0] // 2

    def regroup(xs, m):
        moved = [x if r == m else pltpu.roll(x, (TOPK * (r - m)) % LANES, 1) for r, x in enumerate(xs)]
        out = moved[0]
        for r in range(1, 4):
            out = jnp.where(lane == r, moved[r], out)
        return out

    def prepare(tile, slot):
        at = pl.multiple_of(tile * 8, 8)
        for group in range(replicas // 4):
            ks, fs = [], []
            for r in range(4 * group, 4 * group + 4):
                u = all_ref[r, pl.ds(at, 8), :]
                v = all_ref[r, pl.ds(chunks + at, 8), :]
                ks.append((u + factor * v) * (1.0 / replicas))
                fs.append(all_ref[r, pl.ds(2 * chunks + at, 8), :])
            for m in range(4):
                k = regroup(ks, m)
                f = regroup(fs, m).astype(jnp.int32)
                high = k.astype(BF16).astype(F32)
                place = slice(group * LANES, (group + 1) * LANES)
                lists_a[slot, m, :, place] = lax.shift_right_logical(f, 6)
                lists_b[slot, m, :, place] = lax.bitwise_and(f, GROUP - 1)
                lists_h[slot, m, :, place] = high
                lists_l[slot, m, :, place] = k - high

    items = replicas * TOPK
    place = lax.broadcasted_iota(jnp.int32, (GROUP, items), 0)

    def scatter(s, m, slot):
        here = slice(s, s + 1)
        hit = place == lists_a[slot, m, here, :]
        high = jnp.where(hit, lists_h[slot, m, here, :], 0.0).astype(BF16)
        low = jnp.where(hit, lists_l[slot, m, here, :], 0.0).astype(BF16)
        hot = jnp.where(place == lists_b[slot, m, here, :], 1.0, 0.0).astype(BF16)
        out = dot_nt(jnp.concatenate([high, low], axis=0), hot)
        return out[:GROUP] + out[GROUP:]

    def scatter_row(part, s, slot):
        for pair in range(2):
            both = [scatter(4 * part + s, 2 * pair + n, slot) for n in range(2)]
            pooled[part, s * GROUP:(s + 1) * GROUP, pair * LANES:(pair + 1) * LANES] = jnp.concatenate(both, axis=1)

    def inverse_steps(before, last, out):
        table_c, table_r = cols_ref[...], rows_ref[...]
        for n in range(2):
            side = slice(n * LANES, (n + 1) * LANES)
            x = dot(table_r, columns[last, n])
            y = dot(jnp.concatenate(halves(pooled[before, :, side]), axis=1), table_c)
            yield
            update_out[out, last, side, :] = x[:LANES] + x[LANES:]
            high, low = halves(y[:, :LANES] + y[:, LANES:])
            for m in range(2):
                here = slice(m * LANES, (m + 1) * LANES)
                columns[before, m, :LANES, side] = high[here]
                columns[before, m, LANES:, side] = low[here]
            yield

    def update_copy(tile, part):
        top, cols = tile_of(tile)
        there = update_hbm.at[pl.ds(top + part * half, half), cols]
        return pltpu.make_async_copy(update_out.at[tile, part], there, update_sems.at[tile, part])

    def mom_copy(tile):
        return tile_copies(tile, [(mom_hbm, mom_out, True)], mom_sems)[0]

    pooled[1] = jnp.zeros(pooled.shape[1:], F32)
    columns[...] = jnp.zeros_like(columns)
    prepare(0, 0)

    def one(tile, carry):
        slot = tile % 2
        before = jnp.maximum(tile - 1, 0)
        for part in range(2):
            for s, unused in enumerate(inverse_steps(1 - part, part, before)):
                scatter_row(part, s, slot)
        for copy in tile_copies(tile, inward, in_sems):
            copy.wait()
        mom_out[tile] = u_ref[tile] + factor * v_ref[tile]
        prepare(jnp.minimum(tile + 1, 3), 1 - slot)
        mom_copy(tile).start()

        @pl.when(tile > 0)
        def _():
            for part in range(2):
                update_copy(before, part).start()

        return carry

    lax.fori_loop(0, 4, one, 0)
    for part in range(2):
        for unused in inverse_steps(1 - part, part, 3):
            pass
        update_copy(3, part).start()
    for tile in range(4):
        mom_copy(tile).wait()
        for part in range(2):
            update_copy(tile, part).wait()


def body(momentum, gradient, kept_freq, clip_flag):
    replicas, tensors = lax.axis_size("replica"), lax.axis_size("tensor")
    mom, grad, freq = momentum[0], gradient[0], kept_freq[0]
    rows, cols = mom.shape
    chunks = rows // GROUP * cols // GROUP * TOPK // LANES
    stacked, row_table, col_table = (jnp.asarray(t) for t in tables())
    scalar = pl.BlockSpec(memory_space=pltpu.SMEM)
    hbm = pl.BlockSpec(memory_space=pltpu.HBM)
    vmem = pl.BlockSpec(memory_space=pltpu.VMEM)
    limit = pltpu.CompilerParams(vmem_limit_bytes=32 * 1024 * 1024)
    far = lambda x: pltpu.with_memory_space_constraint(x, pltpu.HBM)
    near = lambda x: pltpu.with_memory_space_constraint(x, pltpu.VMEM)

    squares, grad_near, freq_rows = pl.pallas_call(
        square_kernel,
        in_specs=[hbm] * 2,
        out_specs=[hbm, vmem, vmem],
        out_shape=[
            pltpu.HBM((tensors, 8, LANES), F32),
            pltpu.VMEM(grad.shape, BF16),
            pltpu.VMEM((chunks, LANES), jnp.int32),
        ],
        scratch_shapes=[
            pltpu.VMEM(freq.shape, jnp.int32),
            pltpu.VMEM((tensors, 8, LANES), F32),
            pltpu.SemaphoreType.DMA((2,)),
            pltpu.SemaphoreType.DMA((4,)),
        ],
        compiler_params=limit,
    )(far(grad), far(freq))
    squares = lax.all_to_all(squares, "tensor", 0, 0)

    kept, message = pl.pallas_call(
        kept_kernel,
        in_specs=[scalar, hbm, vmem, vmem, vmem],
        out_specs=[vmem, hbm],
        out_shape=[
            pltpu.VMEM((3 * chunks, LANES), F32),
            pltpu.HBM((replicas, 3 * chunks + 8, LANES), F32),
        ],
        scratch_shapes=[
            pltpu.VMEM((4,) + TILE, F32),
            pltpu.VMEM((2, 2 * GROUP, 16 * LANES), BF16),
            pltpu.SemaphoreType.DMA((1, 4)),
            pltpu.SemaphoreType.DMA((replicas,)),
        ],
        compiler_params=limit,
        cost_estimate=pl.CostEstimate(flops=2 * 10 ** 9, bytes_accessed=3 * 2 ** 20, transcendentals=0),
    )(clip_flag, far(mom), near(grad_near), near(freq_rows), near(stacked))

    message = pl.pallas_call(
        message_kernel,
        in_specs=[hbm, vmem],
        out_specs=hbm,
        out_shape=pltpu.HBM(message.shape, F32),
        input_output_aliases={0: 0},
        scratch_shapes=[pltpu.VMEM((8, LANES), F32), pltpu.SemaphoreType.DMA((replicas,))],
        compiler_params=limit,
    )(far(message), near(squares))
    everyone = lax.all_to_all(message, "replica", 0, 0)

    own_u, own_v = pl.pallas_call(
        own_kernel,
        in_specs=[scalar, hbm, hbm, vmem, vmem],
        out_specs=[hbm] * 2,
        out_shape=[pltpu.HBM((rows, cols), F32)] * 2,
        scratch_shapes=[pltpu.VMEM((4,) + TILE, t) for t in (F32, BF16, F32, F32)] + [pltpu.SemaphoreType.DMA((2, 4))] * 2,
        compiler_params=limit,
        cost_estimate=pl.CostEstimate(flops=2 * 10 ** 9, bytes_accessed=7 * 2 ** 20, transcendentals=0),
    )(clip_flag, far(mom), far(grad), near(kept), near(stacked))

    new_mom, update = pl.pallas_call(
        lambda *refs: update_kernel(replicas * tensors * rows * cols, *refs),
        in_specs=[vmem, hbm, hbm, vmem, vmem],
        out_specs=[hbm] * 2,
        out_shape=[jax.ShapeDtypeStruct((rows, cols), F32)] * 2,
        scratch_shapes=[pltpu.VMEM((2, 4, 8, replicas * TOPK), t) for t in (jnp.int32, jnp.int32, F32, F32)]
        + [
            pltpu.VMEM((2, TILE[0] // 2, TILE[1]), F32),
            pltpu.VMEM((2, 2, TILE[0] // 2, TILE[1]), BF16),
            pltpu.VMEM((4,) + TILE, F32),
            pltpu.VMEM((4,) + TILE, F32),
            pltpu.VMEM((4,) + TILE, F32),
            pltpu.VMEM((4, 2, TILE[0] // 2, TILE[1]), F32),
            pltpu.SemaphoreType.DMA((2, 4)),
            pltpu.SemaphoreType.DMA((1, 4)),
            pltpu.SemaphoreType.DMA((4, 2)),
        ],
        compiler_params=limit,
    )(near(everyone), far(own_u), far(own_v), near(row_table), near(col_table))
    return (new_mom[None], update)


def solution(mesh):
    placed = (
        P("replica", None, "tensor"),
        P("replica", None, "tensor"),
        P("replica", None, "tensor", None),
        P("replica"),
    )
    return jax.shard_map(
        body,
        mesh=mesh,
        in_specs=placed,
        out_specs=(P("replica", None, "tensor"), P(None, "tensor")),
        check_vma=False,
    )
```

```python
import math

import jax
import jax.numpy as jnp
import ml_dtypes
import numpy as np
from jax import lax
from jax.experimental import pallas as pl
from jax.experimental.pallas import tpu as pltpu
from jax.sharding import PartitionSpec as P

GROUP = 64
TOPK = 32
LANES = 128
TILE = (512, 256)
CLIP_RMS = 0.5
DECAY = 0.9
F32 = jnp.float32
BF16 = jnp.bfloat16


def split_table(table):
    high = table.astype(ml_dtypes.bfloat16)
    low = (table - high.astype(np.float64)).astype(ml_dtypes.bfloat16)
    return high, low


def tables():
    freq = np.arange(GROUP)[:, None]
    place = np.arange(GROUP)[None, :]
    table = np.sqrt(np.where(freq == 0, 1.0, 2.0) / GROUP) * np.cos(math.pi * (2 * place + 1) * freq / (2 * GROUP))
    high, low = split_table(table)
    stacked = np.concatenate([high.T, low.T], axis=0)
    pair = [np.kron(np.eye(2), t.astype(np.float64)) for t in (high, low)]
    none = np.zeros_like(pair[0])
    cols = np.block([[pair[0], pair[1]], [pair[0], none]]).astype(ml_dtypes.bfloat16)
    rows = np.block([[pair[0].T, pair[0].T], [pair[1].T, none]]).astype(ml_dtypes.bfloat16)
    return stacked, rows, cols


def halves(x):
    high = x.astype(BF16)
    return high, (x - high.astype(F32)).astype(BF16)


def dot(a, b):
    return jnp.dot(a, b, preferred_element_type=F32)


def dot_nt(a, b):
    return lax.dot_general(a, b, (((1,), (1,)), ((), ())), preferred_element_type=F32)


def square_kernel(grad_hbm, freq_hbm, square_hbm, grad_ref, freq_rows, freq_ref, squares, sems, grad_sems):
    pieces = 4
    rows = grad_ref.shape[0] // pieces
    small = pltpu.make_async_copy(freq_hbm, freq_ref, sems.at[0])
    large = []
    for n in range(pieces):
        here = pl.ds(n * rows, rows)
        large.append(pltpu.make_async_copy(grad_hbm.at[here], grad_ref.at[here], grad_sems.at[n]))
    for copy in large + [small]:
        copy.start()
    part = jnp.zeros((8, LANES), F32)
    for n, copy in enumerate(large):
        copy.wait()
        g = grad_ref[n * rows:(n + 1) * rows, :].astype(F32)
        g = g * g
        g = g.reshape(-1, 8, g.shape[1]).sum(axis=0)
        part += sum(g[:, m * LANES:(m + 1) * LANES] for m in range(g.shape[1] // LANES))
    for n in range(squares.shape[0]):
        squares[n] = part
    result = pltpu.make_async_copy(squares, square_hbm, sems.at[1])
    result.start()
    small.wait()
    for col in range(2):
        freq_rows[16 * col:16 * col + 16, :] = jnp.concatenate([freq_ref[:, 4 * col + m, :] for m in range(4)], axis=1)
    result.wait()


def table_rows(freqs, stacked):
    places, wide = [], freqs.shape[0] * LANES
    for n in (0, 1):
        index = lax.shift_right_logical(freqs, 6) if n == 0 else lax.bitwise_and(freqs, GROUP - 1)
        places += [index[s:s + 1, :] for s in range(freqs.shape[0])]
    row = lax.broadcasted_iota(jnp.int32, (GROUP, 2 * wide), 0)
    hot = jnp.where(row == jnp.concatenate(places, axis=1), 1.0, 0.0).astype(BF16)
    return dot(stacked, hot).astype(BF16)


def parts(table, s):
    a = slice(s * LANES, (s + 1) * LANES)
    b = slice((s + 8) * LANES, (s + 9) * LANES)
    return table[:GROUP, a], table[GROUP:, a], table[:GROUP, b], table[GROUP:, b]


def diagonal(x):
    lane = lax.broadcasted_iota(jnp.int32, x.shape, 1)
    zero = jnp.zeros_like(x)
    return jnp.concatenate([jnp.where(lane // TOPK == m, x, zero) for m in range(4)], axis=0)


def tile_of(step):
    return pl.multiple_of(step % 2 * TILE[0], TILE[0]), pl.ds(pl.multiple_of(step // 2 * TILE[1], TILE[1]), TILE[1])


def tile_copies(step, pairs, sems):
    top, cols = tile_of(step)
    out = []
    for n, (hbm, tiles, outward) in enumerate(pairs):
        far, near = hbm.at[pl.ds(top, TILE[0]), cols], tiles.at[step]
        out.append(pltpu.make_async_copy(near if outward else far, far if outward else near, sems.at[n, step]))
    return out


def kept_kernel(flag_ref, mom_hbm, grad_ref, freq_rows, stacked_ref, out_ref, message_hbm, mom, table, in_sems, out_sems):
    inward = [(mom_hbm, mom, False)]
    for step in range(4):
        for copy in tile_copies(step, inward, in_sems):
            copy.start()
    flag = (flag_ref[0] == 1).astype(F32)
    stacked = stacked_ref[...]
    chunks = freq_rows.shape[0]
    table[0] = table_rows(freq_rows[:8, :], stacked)

    def one(step, carry):
        at = pl.multiple_of(step * 8, 8)
        later = pl.multiple_of(jnp.minimum(step + 1, 3) * 8, 8)
        top, cols = tile_of(step)
        freqs = freq_rows[pl.ds(at, 8), :]
        for copy in tile_copies(step, inward, in_sems):
            copy.wait()
        us, vs = [], []
        for s in range(8):
            rows = slice(s * GROUP, (s + 1) * GROUP)
            ah, al, bh, bl = parts(table.at[step % 2], s)
            weights = jnp.concatenate([diagonal(bh), diagonal(bl)], axis=1)
            xh, xl = halves(mom[step, rows, :])
            y = dot(jnp.concatenate([xh, xl, grad_ref[pl.ds(top + s * GROUP, GROUP), cols]], axis=0), weights)
            y = y[:, :LANES] + y[:, LANES:]
            a = ah.astype(F32) + al.astype(F32)
            km = jnp.sum((y[:GROUP] + y[GROUP:2 * GROUP]) * a, axis=0, keepdims=True)
            kg = jnp.sum(y[2 * GROUP:] * a, axis=0, keepdims=True)
            us.append(DECAY * km + (1.0 - flag) * kg)
            vs.append(flag * kg)
        table[(step + 1) % 2] = table_rows(freq_rows[pl.ds(later, 8), :], stacked)
        out_ref[pl.ds(at, 8), :] = jnp.concatenate(us, axis=0)
        out_ref[pl.ds(chunks + at, 8), :] = jnp.concatenate(vs, axis=0)
        out_ref[pl.ds(2 * chunks + at, 8), :] = freqs.astype(F32)
        return carry

    lax.fori_loop(0, 4, one, 0)
    copies = [
        pltpu.make_async_copy(out_ref, message_hbm.at[n, pl.ds(0, 3 * chunks)], out_sems.at[n])
        for n in range(message_hbm.shape[0])
    ]
    for copy in copies:
        copy.start()
    for copy in copies:
        copy.wait()


def message_kernel(message_hbm, square_ref, out_hbm, total, sems):
    total[...] = jnp.sum(square_ref[...], axis=0)
    replicas, rows = out_hbm.shape[:2]
    copies = [pltpu.make_async_copy(total, out_hbm.at[n, pl.ds(rows - 8, 8)], sems.at[n]) for n in range(replicas)]
    for copy in copies:
        copy.start()
    for copy in copies:
        copy.wait()


def own_kernel(flag_ref, mom_hbm, grad_hbm, kept_ref, stacked_ref, u_hbm, v_hbm, mom, grad, u_out, v_out, in_sems, out_sems):
    inward = [(mom_hbm, mom, False), (grad_hbm, grad, False)]
    outward = [(u_hbm, u_out, True), (v_hbm, v_out, True)]
    for step in range(4):
        for copy in tile_copies(step, inward, in_sems):
            copy.start()
    flag = (flag_ref[0] == 1).astype(F32)
    stacked = stacked_ref[...]
    chunks = kept_ref.shape[0] // 3

    def one(step, carry):
        at = pl.multiple_of(step * 8, 8)
        us = kept_ref[pl.ds(at, 8), :]
        vs = kept_ref[pl.ds(chunks + at, 8), :]
        table = table_rows(kept_ref[pl.ds(2 * chunks + at, 8), :].astype(jnp.int32), stacked)
        for copy in tile_copies(step, inward, in_sems):
            copy.wait()
        for s in range(8):
            rows = slice(s * GROUP, (s + 1) * GROUP)
            ah, al, bh, bl = parts(table, s)
            a = ah.astype(F32) + al.astype(F32)
            high, low = halves(jnp.concatenate([a * us[s:s + 1, :], a * vs[s:s + 1, :]], axis=0))
            left = jnp.concatenate([high, low], axis=0)
            right = jnp.concatenate([high, jnp.zeros_like(low)], axis=0)
            y = dot_nt(jnp.concatenate([left, right], axis=1), jnp.concatenate([diagonal(bh), diagonal(bl)], axis=1))
            g = grad[step, rows, :].astype(F32)
            u_out[step, rows, :] = DECAY * mom[step, rows, :] + (1.0 - flag) * g - (y[:GROUP] + y[2 * GROUP:3 * GROUP])
            v_out[step, rows, :] = flag * g - (y[GROUP:2 * GROUP] + y[3 * GROUP:])
        for copy in tile_copies(step, outward, out_sems):
            copy.start()
        return carry

    lax.fori_loop(0, 4, one, 0)
    for step in range(4):
        for copy in tile_copies(step, outward, out_sems):
            copy.wait()


def update_kernel(count, all_ref, u_hbm, v_hbm, rows_ref, cols_ref, mom_hbm, update_hbm, lists_a, lists_b, lists_h, lists_l, pooled, columns,
                  u_ref, v_ref, mom_out, update_out, in_sems, mom_sems, update_sems):
    inward = [(u_hbm, u_ref, False), (v_hbm, v_ref, False)]
    for tile in range(4):
        for copy in tile_copies(tile, inward, in_sems):
            copy.start()
    replicas = all_ref.shape[0]
    chunks = (all_ref.shape[1] - 8) // 3
    total = jnp.sum(all_ref[:, 3 * chunks:, :], axis=0)
    total = jnp.sum(total, axis=(0, 1), keepdims=True)
    rms = jnp.sqrt(total * (1.0 / count))
    factor = jnp.minimum(jnp.float32(1.0), CLIP_RMS / (rms + 1e-06))
    lane = lax.broadcasted_iota(jnp.int32, (8, LANES), 1) // TOPK
    half = TILE[0] // 2

    def regroup(xs, m):
        moved = [x if r == m else pltpu.roll(x, (TOPK * (r - m)) % LANES, 1) for r, x in enumerate(xs)]
        out = moved[0]
        for r in range(1, 4):
            out = jnp.where(lane == r, moved[r], out)
        return out

    def prepare(tile, slot):
        at = pl.multiple_of(tile * 8, 8)
        for group in range(replicas // 4):
            ks, fs = [], []
            for r in range(4 * group, 4 * group + 4):
                u = all_ref[r, pl.ds(at, 8), :]
                v = all_ref[r, pl.ds(chunks + at, 8), :]
                ks.append((u + factor * v) * (1.0 / replicas))
                fs.append(all_ref[r, pl.ds(2 * chunks + at, 8), :])
            for m in range(4):
                k = regroup(ks, m)
                f = regroup(fs, m)
                a = jnp.floor(f * (1.0 / GROUP))
                high = k.astype(BF16).astype(F32)
                place = slice(group * LANES, (group + 1) * LANES)
                lists_a[slot, m, :, place] = a
                lists_b[slot, m, :, place] = f - a * GROUP
                lists_h[slot, m, :, place] = high
                lists_l[slot, m, :, place] = k - high

    items = replicas * TOPK
    place = lax.broadcasted_iota(jnp.int32, (GROUP, items), 0).astype(F32).astype(BF16)
    zero = jnp.zeros((), BF16)

    def scatter(s, m, slot):
        here = slice(s, s + 1)
        a, b, h, l = (x[slot, m, here, :].astype(BF16) for x in (lists_a, lists_b, lists_h, lists_l))
        hit = place == a
        high = jnp.where(hit, h, zero)
        low = jnp.where(hit, l, zero)
        hot = jnp.where(place == b, jnp.ones((), BF16), zero)
        out = dot_nt(jnp.concatenate([high, low], axis=0), hot)
        return out[:GROUP] + out[GROUP:]

    def scatter_row(part, s, slot):
        for pair in range(2):
            both = [scatter(4 * part + s, 2 * pair + n, slot) for n in range(2)]
            pooled[part, s * GROUP:(s + 1) * GROUP, pair * LANES:(pair + 1) * LANES] = jnp.concatenate(both, axis=1)

    def inverse_steps(before, last, out, final=False):
        table_c, table_r = cols_ref[...], rows_ref[...]
        for n in range(2):
            side = slice(n * LANES, (n + 1) * LANES)
            x = dot(table_r, columns[last, n])
            if not final:
                y = dot(jnp.concatenate(halves(pooled[before, :, side]), axis=1), table_c)
            yield
            update_out[out, last, side, :] = x[:LANES] + x[LANES:]
            if final:
                continue
            high, low = halves(y[:, :LANES] + y[:, LANES:])
            for m in range(2):
                here = slice(m * LANES, (m + 1) * LANES)
                columns[before, m, :LANES, side] = high[here]
                columns[before, m, LANES:, side] = low[here]
            yield

    def update_copy(tile, part):
        top, cols = tile_of(tile)
        there = update_hbm.at[pl.ds(top + part * half, half), cols]
        return pltpu.make_async_copy(update_out.at[tile, part], there, update_sems.at[tile, part])

    def mom_copy(tile):
        return tile_copies(tile, [(mom_hbm, mom_out, True)], mom_sems)[0]

    pooled[1] = jnp.zeros(pooled.shape[1:], F32)
    columns[...] = jnp.zeros_like(columns)
    prepare(0, 0)

    def one(tile, carry):
        slot = tile % 2
        before = jnp.maximum(tile - 1, 0)
        prepare(jnp.minimum(tile + 1, 3), 1 - slot)
        for part in range(2):
            for s, unused in enumerate(inverse_steps(1 - part, part, before)):
                scatter_row(part, s, slot)
        for copy in tile_copies(tile, inward, in_sems):
            copy.wait()
        mom_out[tile] = u_ref[tile] + factor * v_ref[tile]
        mom_copy(tile).start()

        @pl.when(tile > 0)
        def _():
            for part in range(2):
                update_copy(before, part).start()

        return carry

    lax.fori_loop(0, 4, one, 0)
    for part in range(2):
        for unused in inverse_steps(1 - part, part, 3, final=part == 1):
            pass
        update_copy(3, part).start()
    for tile in range(4):
        mom_copy(tile).wait()
        for part in range(2):
            update_copy(tile, part).wait()


def body(momentum, gradient, kept_freq, clip_flag):
    replicas, tensors = lax.axis_size("replica"), lax.axis_size("tensor")
    mom, grad, freq = momentum[0], gradient[0], kept_freq[0]
    rows, cols = mom.shape
    chunks = rows // GROUP * cols // GROUP * TOPK // LANES
    stacked, row_table, col_table = (jnp.asarray(t) for t in tables())
    scalar = pl.BlockSpec(memory_space=pltpu.SMEM)
    hbm = pl.BlockSpec(memory_space=pltpu.HBM)
    vmem = pl.BlockSpec(memory_space=pltpu.VMEM)
    limit = pltpu.CompilerParams(vmem_limit_bytes=32 * 1024 * 1024)
    far = lambda x: pltpu.with_memory_space_constraint(x, pltpu.HBM)
    near = lambda x: pltpu.with_memory_space_constraint(x, pltpu.VMEM)

    squares, grad_near, freq_rows = pl.pallas_call(
        square_kernel,
        in_specs=[hbm] * 2,
        out_specs=[hbm, vmem, vmem],
        out_shape=[
            pltpu.HBM((tensors, 8, LANES), F32),
            pltpu.VMEM(grad.shape, BF16),
            pltpu.VMEM((chunks, LANES), jnp.int32),
        ],
        scratch_shapes=[
            pltpu.VMEM(freq.shape, jnp.int32),
            pltpu.VMEM((tensors, 8, LANES), F32),
            pltpu.SemaphoreType.DMA((2,)),
            pltpu.SemaphoreType.DMA((4,)),
        ],
        compiler_params=limit,
    )(far(grad), far(freq))
    squares = lax.all_to_all(squares, "tensor", 0, 0)

    kept, message = pl.pallas_call(
        kept_kernel,
        in_specs=[scalar, hbm, vmem, vmem, vmem],
        out_specs=[vmem, hbm],
        out_shape=[
            pltpu.VMEM((3 * chunks, LANES), F32),
            pltpu.HBM((replicas, 3 * chunks + 8, LANES), F32),
        ],
        scratch_shapes=[
            pltpu.VMEM((4,) + TILE, F32),
            pltpu.VMEM((2, 2 * GROUP, 16 * LANES), BF16),
            pltpu.SemaphoreType.DMA((1, 4)),
            pltpu.SemaphoreType.DMA((replicas,)),
        ],
        compiler_params=limit,
        cost_estimate=pl.CostEstimate(flops=2 * 10 ** 9, bytes_accessed=3 * 2 ** 20, transcendentals=0),
    )(clip_flag, far(mom), near(grad_near), near(freq_rows), near(stacked))

    message = pl.pallas_call(
        message_kernel,
        in_specs=[hbm, vmem],
        out_specs=hbm,
        out_shape=pltpu.HBM(message.shape, F32),
        input_output_aliases={0: 0},
        scratch_shapes=[pltpu.VMEM((8, LANES), F32), pltpu.SemaphoreType.DMA((replicas,))],
        compiler_params=limit,
    )(far(message), near(squares))
    everyone = lax.all_to_all(message, "replica", 0, 0)

    own_u, own_v = pl.pallas_call(
        own_kernel,
        in_specs=[scalar, hbm, hbm, vmem, vmem],
        out_specs=[hbm] * 2,
        out_shape=[pltpu.HBM((rows, cols), F32)] * 2,
        scratch_shapes=[pltpu.VMEM((4,) + TILE, t) for t in (F32, BF16, F32, F32)] + [pltpu.SemaphoreType.DMA((2, 4))] * 2,
        compiler_params=limit,
        cost_estimate=pl.CostEstimate(flops=2 * 10 ** 9, bytes_accessed=7 * 2 ** 20, transcendentals=0),
    )(clip_flag, far(mom), far(grad), near(kept), near(stacked))

    new_mom, update = pl.pallas_call(
        lambda *refs: update_kernel(replicas * tensors * rows * cols, *refs),
        in_specs=[vmem, hbm, hbm, vmem, vmem],
        out_specs=[hbm] * 2,
        out_shape=[jax.ShapeDtypeStruct((rows, cols), F32)] * 2,
        scratch_shapes=[pltpu.VMEM((2, 4, 8, replicas * TOPK), t) for t in (F32,) * 4]
        + [
            pltpu.VMEM((2, TILE[0] // 2, TILE[1]), F32),
            pltpu.VMEM((2, 2, TILE[0] // 2, TILE[1]), BF16),
            pltpu.VMEM((4,) + TILE, F32),
            pltpu.VMEM((4,) + TILE, F32),
            pltpu.VMEM((4,) + TILE, F32),
            pltpu.VMEM((4, 2, TILE[0] // 2, TILE[1]), F32),
            pltpu.SemaphoreType.DMA((2, 4)),
            pltpu.SemaphoreType.DMA((1, 4)),
            pltpu.SemaphoreType.DMA((4, 2)),
        ],
        compiler_params=limit,
    )(near(everyone), far(own_u), far(own_v), near(row_table), near(col_table))
    return (new_mom[None], update)


def solution(mesh):
    placed = (
        P("replica", None, "tensor"),
        P("replica", None, "tensor"),
        P("replica", None, "tensor", None),
        P("replica"),
    )
    return jax.shard_map(
        body,
        mesh=mesh,
        in_specs=placed,
        out_specs=(P("replica", None, "tensor"), P(None, "tensor")),
        check_vma=False,
    )
```

```python
import math

import jax
import jax.numpy as jnp
import ml_dtypes
import numpy as np
from jax import lax
from jax.experimental import pallas as pl
from jax.experimental.pallas import tpu as pltpu
from jax.sharding import PartitionSpec as P

GROUP = 64
TOPK = 32
LANES = 128
TILE = (512, 256)
CLIP_RMS = 0.5
DECAY = 0.9
F32 = jnp.float32
BF16 = jnp.bfloat16


def split_table(table):
    high = table.astype(ml_dtypes.bfloat16)
    low = (table - high.astype(np.float64)).astype(ml_dtypes.bfloat16)
    return high, low


def tables():
    freq = np.arange(GROUP)[:, None]
    place = np.arange(GROUP)[None, :]
    table = np.sqrt(np.where(freq == 0, 1.0, 2.0) / GROUP) * np.cos(math.pi * (2 * place + 1) * freq / (2 * GROUP))
    high, low = split_table(table)
    stacked = np.concatenate([high.T, low.T], axis=0)
    pair = [np.kron(np.eye(2), t.astype(np.float64)) for t in (high, low)]
    none = np.zeros_like(pair[0])
    cols = np.block([[pair[0], pair[1]], [pair[0], none]]).astype(ml_dtypes.bfloat16)
    rows = np.block([[pair[0].T, pair[0].T], [pair[1].T, none]]).astype(ml_dtypes.bfloat16)
    return stacked, rows, cols


def halves(x):
    high = x.astype(BF16)
    return high, (x - high.astype(F32)).astype(BF16)


def dot(a, b):
    return jnp.dot(a, b, preferred_element_type=F32)


def dot_nt(a, b):
    return lax.dot_general(a, b, (((1,), (1,)), ((), ())), preferred_element_type=F32)


def square_kernel(grad_hbm, freq_hbm, square_hbm, grad_ref, freq_rows, freq_ref, squares, sems, grad_sems):
    pieces = 4
    rows = grad_ref.shape[0] // pieces
    small = pltpu.make_async_copy(freq_hbm, freq_ref, sems.at[0])
    large = []
    for n in range(pieces):
        here = pl.ds(n * rows, rows)
        large.append(pltpu.make_async_copy(grad_hbm.at[here], grad_ref.at[here], grad_sems.at[n]))
    for copy in large + [small]:
        copy.start()
    part = jnp.zeros((8, LANES), F32)
    for n, copy in enumerate(large):
        copy.wait()
        g = grad_ref[n * rows:(n + 1) * rows, :].astype(F32)
        g = g * g
        g = g.reshape(-1, 8, g.shape[1]).sum(axis=0)
        part += sum(g[:, m * LANES:(m + 1) * LANES] for m in range(g.shape[1] // LANES))
    for n in range(squares.shape[0]):
        squares[n] = part
    result = pltpu.make_async_copy(squares, square_hbm, sems.at[1])
    result.start()
    small.wait()
    for col in range(2):
        freq_rows[16 * col:16 * col + 16, :] = jnp.concatenate([freq_ref[:, 4 * col + m, :] for m in range(4)], axis=1)
    result.wait()


def table_rows(freqs, stacked):
    places, wide = [], freqs.shape[0] * LANES
    for n in (0, 1):
        index = lax.shift_right_logical(freqs, 6) if n == 0 else lax.bitwise_and(freqs, GROUP - 1)
        places += [index[s:s + 1, :] for s in range(freqs.shape[0])]
    row = lax.broadcasted_iota(jnp.int32, (GROUP, 2 * wide), 0)
    hot = jnp.where(row == jnp.concatenate(places, axis=1), 1.0, 0.0).astype(BF16)
    return dot(stacked, hot).astype(BF16)


def parts(table, s):
    a = slice(s * LANES, (s + 1) * LANES)
    b = slice((s + 8) * LANES, (s + 9) * LANES)
    return table[:GROUP, a], table[GROUP:, a], table[:GROUP, b], table[GROUP:, b]


def diagonal(x):
    lane = lax.broadcasted_iota(jnp.int32, x.shape, 1)
    zero = jnp.zeros_like(x)
    return jnp.concatenate([jnp.where(lane // TOPK == m, x, zero) for m in range(4)], axis=0)


def tile_of(step):
    return pl.multiple_of(step % 2 * TILE[0], TILE[0]), pl.ds(pl.multiple_of(step // 2 * TILE[1], TILE[1]), TILE[1])


def tile_copies(step, pairs, sems):
    top, cols = tile_of(step)
    out = []
    for n, (hbm, tiles, outward) in enumerate(pairs):
        far, near = hbm.at[pl.ds(top, TILE[0]), cols], tiles.at[step]
        out.append(pltpu.make_async_copy(near if outward else far, far if outward else near, sems.at[n, step]))
    return out


def kept_kernel(flag_ref, mom_hbm, grad_ref, freq_rows, stacked_ref, out_ref, message_hbm, mom, table, in_sems, out_sems):
    inward = [(mom_hbm, mom, False)]
    for step in range(4):
        for copy in tile_copies(step, inward, in_sems):
            copy.start()
    flag = (flag_ref[0] == 1).astype(F32)
    stacked = stacked_ref[...]
    chunks = freq_rows.shape[0]
    table[0] = table_rows(freq_rows[:8, :], stacked)

    def one(step, carry):
        at = pl.multiple_of(step * 8, 8)
        later = pl.multiple_of(jnp.minimum(step + 1, 3) * 8, 8)
        top, cols = tile_of(step)
        freqs = freq_rows[pl.ds(at, 8), :]
        for copy in tile_copies(step, inward, in_sems):
            copy.wait()
        us, vs = [], []
        for s in range(8):
            rows = slice(s * GROUP, (s + 1) * GROUP)
            ah, al, bh, bl = parts(table.at[step % 2], s)
            weights = jnp.concatenate([diagonal(bh), diagonal(bl)], axis=1)
            xh, xl = halves(mom[step, rows, :])
            y = dot(jnp.concatenate([xh, xl, grad_ref[pl.ds(top + s * GROUP, GROUP), cols]], axis=0), weights)
            y = y[:, :LANES] + y[:, LANES:]
            a = ah.astype(F32) + al.astype(F32)
            km = jnp.sum((y[:GROUP] + y[GROUP:2 * GROUP]) * a, axis=0, keepdims=True)
            kg = jnp.sum(y[2 * GROUP:] * a, axis=0, keepdims=True)
            us.append(DECAY * km + (1.0 - flag) * kg)
            vs.append(flag * kg)
        table[(step + 1) % 2] = table_rows(freq_rows[pl.ds(later, 8), :], stacked)
        out_ref[pl.ds(at, 8), :] = jnp.concatenate(us, axis=0)
        out_ref[pl.ds(chunks + at, 8), :] = jnp.concatenate(vs, axis=0)
        out_ref[pl.ds(2 * chunks + at, 8), :] = freqs.astype(F32)
        return carry

    lax.fori_loop(0, 4, one, 0)
    copies = [
        pltpu.make_async_copy(out_ref, message_hbm.at[n, pl.ds(0, 3 * chunks)], out_sems.at[n])
        for n in range(message_hbm.shape[0])
    ]
    for copy in copies:
        copy.start()
    for copy in copies:
        copy.wait()


def message_kernel(message_hbm, square_ref, out_hbm, total, sems):
    total[...] = jnp.sum(square_ref[...], axis=0)
    replicas, rows = out_hbm.shape[:2]
    copies = [pltpu.make_async_copy(total, out_hbm.at[n, pl.ds(rows - 8, 8)], sems.at[n]) for n in range(replicas)]
    for copy in copies:
        copy.start()
    for copy in copies:
        copy.wait()


def own_kernel(flag_ref, mom_hbm, grad_hbm, kept_ref, stacked_ref, u_hbm, v_hbm, mom, grad, u_out, v_out, in_sems, out_sems):
    inward = [(mom_hbm, mom, False), (grad_hbm, grad, False)]
    outward = [(u_hbm, u_out, True), (v_hbm, v_out, True)]
    for step in range(4):
        for copy in tile_copies(step, inward, in_sems):
            copy.start()
    flag = (flag_ref[0] == 1).astype(F32)
    stacked = stacked_ref[...]
    chunks = kept_ref.shape[0] // 3

    def one(step, carry):
        at = pl.multiple_of(step * 8, 8)
        us = kept_ref[pl.ds(at, 8), :]
        vs = kept_ref[pl.ds(chunks + at, 8), :]
        table = table_rows(kept_ref[pl.ds(2 * chunks + at, 8), :].astype(jnp.int32), stacked)
        for copy in tile_copies(step, inward, in_sems):
            copy.wait()
        for s in range(8):
            rows = slice(s * GROUP, (s + 1) * GROUP)
            ah, al, bh, bl = parts(table, s)
            a = ah.astype(F32) + al.astype(F32)
            high, low = halves(jnp.concatenate([a * us[s:s + 1, :], a * vs[s:s + 1, :]], axis=0))
            left = jnp.concatenate([high, low], axis=0)
            right = jnp.concatenate([high, jnp.zeros_like(low)], axis=0)
            y = dot_nt(jnp.concatenate([left, right], axis=1), jnp.concatenate([diagonal(bh), diagonal(bl)], axis=1))
            g = grad[step, rows, :].astype(F32)
            u_out[step, rows, :] = DECAY * mom[step, rows, :] + (1.0 - flag) * g - (y[:GROUP] + y[2 * GROUP:3 * GROUP])
            v_out[step, rows, :] = flag * g - (y[GROUP:2 * GROUP] + y[3 * GROUP:])
        for copy in tile_copies(step, outward, out_sems):
            copy.start()
        return carry

    lax.fori_loop(0, 4, one, 0)
    for step in range(4):
        for copy in tile_copies(step, outward, out_sems):
            copy.wait()


def update_kernel(count, all_ref, u_hbm, v_hbm, rows_ref, cols_ref, mom_hbm, update_hbm, lists_a, lists_b, lists_h, lists_l, pooled, columns,
                  u_ref, v_ref, mom_out, update_out, in_sems, mom_sems, update_sems):
    inward = [(u_hbm, u_ref, False), (v_hbm, v_ref, False)]
    for tile in range(4):
        for copy in tile_copies(tile, inward, in_sems):
            copy.start()
    replicas = all_ref.shape[0]
    chunks = (all_ref.shape[1] - 8) // 3
    total = jnp.sum(all_ref[:, 3 * chunks:, :], axis=0)
    total = jnp.sum(total, axis=(0, 1), keepdims=True)
    rms = jnp.sqrt(total * (1.0 / count))
    factor = jnp.minimum(jnp.float32(1.0), CLIP_RMS / (rms + 1e-06))
    lane = lax.broadcasted_iota(jnp.int32, (8, LANES), 1) // TOPK
    half = TILE[0] // 2

    def regroup(xs, m):
        moved = [x if r == m else pltpu.roll(x, (TOPK * (r - m)) % LANES, 1) for r, x in enumerate(xs)]
        out = moved[0]
        for r in range(1, 4):
            out = jnp.where(lane == r, moved[r], out)
        return out

    def prepare(tile, slot):
        at = pl.multiple_of(tile * 8, 8)
        for group in range(replicas // 4):
            ks, fs = [], []
            for r in range(4 * group, 4 * group + 4):
                u = all_ref[r, pl.ds(at, 8), :]
                v = all_ref[r, pl.ds(chunks + at, 8), :]
                ks.append((u + factor * v) * (1.0 / replicas))
                fs.append(all_ref[r, pl.ds(2 * chunks + at, 8), :])
            for m in range(4):
                k = regroup(ks, m)
                f = regroup(fs, m)
                a = jnp.floor(f * (1.0 / GROUP))
                high = k.astype(BF16).astype(F32)
                place = slice(group * LANES, (group + 1) * LANES)
                lists_a[slot, m, :, place] = a
                lists_b[slot, m, :, place] = f - a * GROUP
                lists_h[slot, m, :, place] = high
                lists_l[slot, m, :, place] = k - high

    items = replicas * TOPK
    place = lax.broadcasted_iota(jnp.int32, (GROUP, items), 0).astype(F32).astype(BF16)
    zero = jnp.zeros((), BF16)

    def scatter(s, m, slot):
        here = slice(s, s + 1)
        a, b, h, l = (x[slot, m, here, :].astype(BF16) for x in (lists_a, lists_b, lists_h, lists_l))
        hit = place == a
        high = jnp.where(hit, h, zero)
        low = jnp.where(hit, l, zero)
        hot = jnp.where(place == b, jnp.ones((), BF16), zero)
        out = dot_nt(jnp.concatenate([high, low], axis=0), hot)
        return out[:GROUP] + out[GROUP:]

    def scatter_row(part, s, slot):
        for pair in range(2):
            both = [scatter(4 * part + s, 2 * pair + n, slot) for n in range(2)]
            pooled[part, s * GROUP:(s + 1) * GROUP, pair * LANES:(pair + 1) * LANES] = jnp.concatenate(both, axis=1)

    def inverse_steps(before, last, out, final=False):
        table_c, table_r = cols_ref[...], rows_ref[...]
        for n in range(2):
            side = slice(n * LANES, (n + 1) * LANES)
            x = dot(table_r, columns[last, n])
            if not final:
                y = dot(jnp.concatenate(halves(pooled[before, :, side]), axis=1), table_c)
            yield
            update_out[out, last, side, :] = x[:LANES] + x[LANES:]
            if final:
                continue
            high, low = halves(y[:, :LANES] + y[:, LANES:])
            for m in range(2):
                here = slice(m * LANES, (m + 1) * LANES)
                columns[before, m, :LANES, side] = high[here]
                columns[before, m, LANES:, side] = low[here]
            yield

    def update_copy(tile, part):
        top, cols = tile_of(tile)
        there = update_hbm.at[pl.ds(top + part * half, half), cols]
        return pltpu.make_async_copy(update_out.at[tile, part], there, update_sems.at[tile, part])

    def mom_copy(tile):
        return tile_copies(tile, [(mom_hbm, mom_out, True)], mom_sems)[0]

    pooled[1] = jnp.zeros(pooled.shape[1:], F32)
    columns[...] = jnp.zeros_like(columns)
    prepare(0, 0)

    def one(tile, carry):
        slot = tile % 2
        before = jnp.maximum(tile - 1, 0)
        prepare(jnp.minimum(tile + 1, 3), 1 - slot)
        for part in range(2):
            for s, unused in enumerate(inverse_steps(1 - part, part, before)):
                scatter_row(part, s, slot)
        for copy in tile_copies(tile, inward, in_sems):
            copy.wait()
        mom_out[tile] = u_ref[tile] + factor * v_ref[tile]
        mom_copy(tile).start()

        @pl.when(tile > 0)
        def _():
            for part in range(2):
                update_copy(before, part).start()

        return carry

    lax.fori_loop(0, 4, one, 0)
    for part in range(2):
        for unused in inverse_steps(1 - part, part, 3, final=part == 1):
            pass
        update_copy(3, part).start()
    for tile in range(4):
        mom_copy(tile).wait()
        for part in range(2):
            update_copy(tile, part).wait()


def spread(copies, axis, minor):
    size = lax.axis_size(axis)
    order = sorted(range(size), key=lambda i: (i % minor, i), reverse=True)
    return lax.all_to_all(copies, axis, 0, 0, axis_index_groups=[order])


def body(momentum, gradient, kept_freq, clip_flag):
    replicas, tensors = lax.axis_size("replica"), lax.axis_size("tensor")
    mom, grad, freq = momentum[0], gradient[0], kept_freq[0]
    rows, cols = mom.shape
    chunks = rows // GROUP * cols // GROUP * TOPK // LANES
    stacked, row_table, col_table = (jnp.asarray(t) for t in tables())
    scalar = pl.BlockSpec(memory_space=pltpu.SMEM)
    hbm = pl.BlockSpec(memory_space=pltpu.HBM)
    vmem = pl.BlockSpec(memory_space=pltpu.VMEM)
    limit = pltpu.CompilerParams(vmem_limit_bytes=32 * 1024 * 1024)
    far = lambda x: pltpu.with_memory_space_constraint(x, pltpu.HBM)
    near = lambda x: pltpu.with_memory_space_constraint(x, pltpu.VMEM)

    squares, grad_near, freq_rows = pl.pallas_call(
        square_kernel,
        in_specs=[hbm] * 2,
        out_specs=[hbm, vmem, vmem],
        out_shape=[
            pltpu.HBM((tensors, 8, LANES), F32),
            pltpu.VMEM(grad.shape, BF16),
            pltpu.VMEM((chunks, LANES), jnp.int32),
        ],
        scratch_shapes=[
            pltpu.VMEM(freq.shape, jnp.int32),
            pltpu.VMEM((tensors, 8, LANES), F32),
            pltpu.SemaphoreType.DMA((2,)),
            pltpu.SemaphoreType.DMA((4,)),
        ],
        compiler_params=limit,
    )(far(grad), far(freq))
    squares = spread(squares, "tensor", 2)

    kept, message = pl.pallas_call(
        kept_kernel,
        in_specs=[scalar, hbm, vmem, vmem, vmem],
        out_specs=[vmem, hbm],
        out_shape=[
            pltpu.VMEM((3 * chunks, LANES), F32),
            pltpu.HBM((replicas, 3 * chunks + 8, LANES), F32),
        ],
        scratch_shapes=[
            pltpu.VMEM((4,) + TILE, F32),
            pltpu.VMEM((2, 2 * GROUP, 16 * LANES), BF16),
            pltpu.SemaphoreType.DMA((1, 4)),
            pltpu.SemaphoreType.DMA((replicas,)),
        ],
        compiler_params=limit,
        cost_estimate=pl.CostEstimate(flops=2 * 10 ** 9, bytes_accessed=3 * 2 ** 20, transcendentals=0),
    )(clip_flag, far(mom), near(grad_near), near(freq_rows), near(stacked))

    message = pl.pallas_call(
        message_kernel,
        in_specs=[hbm, vmem],
        out_specs=hbm,
        out_shape=pltpu.HBM(message.shape, F32),
        input_output_aliases={0: 0},
        scratch_shapes=[pltpu.VMEM((8, LANES), F32), pltpu.SemaphoreType.DMA((replicas,))],
        compiler_params=limit,
    )(far(message), near(squares))
    everyone = spread(message, "replica", 4)

    own_u, own_v = pl.pallas_call(
        own_kernel,
        in_specs=[scalar, hbm, hbm, vmem, vmem],
        out_specs=[hbm] * 2,
        out_shape=[pltpu.HBM((rows, cols), F32)] * 2,
        scratch_shapes=[pltpu.VMEM((4,) + TILE, t) for t in (F32, BF16, F32, F32)] + [pltpu.SemaphoreType.DMA((2, 4))] * 2,
        compiler_params=limit,
        cost_estimate=pl.CostEstimate(flops=2 * 10 ** 9, bytes_accessed=7 * 2 ** 20, transcendentals=0),
    )(clip_flag, far(mom), far(grad), near(kept), near(stacked))

    new_mom, update = pl.pallas_call(
        lambda *refs: update_kernel(replicas * tensors * rows * cols, *refs),
        in_specs=[vmem, hbm, hbm, vmem, vmem],
        out_specs=[hbm] * 2,
        out_shape=[jax.ShapeDtypeStruct((rows, cols), F32)] * 2,
        scratch_shapes=[pltpu.VMEM((2, 4, 8, replicas * TOPK), t) for t in (F32,) * 4]
        + [
            pltpu.VMEM((2, TILE[0] // 2, TILE[1]), F32),
            pltpu.VMEM((2, 2, TILE[0] // 2, TILE[1]), BF16),
            pltpu.VMEM((4,) + TILE, F32),
            pltpu.VMEM((4,) + TILE, F32),
            pltpu.VMEM((4,) + TILE, F32),
            pltpu.VMEM((4, 2, TILE[0] // 2, TILE[1]), F32),
            pltpu.SemaphoreType.DMA((2, 4)),
            pltpu.SemaphoreType.DMA((1, 4)),
            pltpu.SemaphoreType.DMA((4, 2)),
        ],
        compiler_params=limit,
    )(near(everyone), far(own_u), far(own_v), near(row_table), near(col_table))
    return (new_mom[None], update)


def solution(mesh):
    placed = (
        P("replica", None, "tensor"),
        P("replica", None, "tensor"),
        P("replica", None, "tensor", None),
        P("replica"),
    )
    return jax.shard_map(
        body,
        mesh=mesh,
        in_specs=placed,
        out_specs=(P("replica", None, "tensor"), P(None, "tensor")),
        check_vma=False,
    )
```

```python
import math

import jax
import jax.numpy as jnp
import ml_dtypes
import numpy as np
from jax import lax
from jax.experimental import pallas as pl
from jax.experimental.pallas import tpu as pltpu
from jax.sharding import PartitionSpec as P

GROUP = 64
TOPK = 32
LANES = 128
TILE = (512, 256)
CLIP_RMS = 0.5
DECAY = 0.9
F32 = jnp.float32
BF16 = jnp.bfloat16


def split_table(table):
    high = table.astype(ml_dtypes.bfloat16)
    low = (table - high.astype(np.float64)).astype(ml_dtypes.bfloat16)
    return high, low


def tables():
    freq = np.arange(GROUP)[:, None]
    place = np.arange(GROUP)[None, :]
    table = np.sqrt(np.where(freq == 0, 1.0, 2.0) / GROUP) * np.cos(math.pi * (2 * place + 1) * freq / (2 * GROUP))
    high, low = split_table(table)
    stacked = np.concatenate([high.T, low.T], axis=0)
    pair = [np.kron(np.eye(2), t.astype(np.float64)) for t in (high, low)]
    none = np.zeros_like(pair[0])
    cols = np.block([[pair[0], pair[1]], [pair[0], none]]).astype(ml_dtypes.bfloat16)
    rows = np.block([[pair[0].T, pair[0].T], [pair[1].T, none]]).astype(ml_dtypes.bfloat16)
    return stacked, rows, cols


def halves(x):
    high = x.astype(BF16)
    return high, (x - high.astype(F32)).astype(BF16)


def dot(a, b):
    return jnp.dot(a, b, preferred_element_type=F32)


def dot_nt(a, b):
    return lax.dot_general(a, b, (((1,), (1,)), ((), ())), preferred_element_type=F32)


def square_kernel(grad_hbm, mom_hbm, freq_hbm, stacked_hbm, square_hbm, grad_ref, mom_ref, freq_rows, stacked_ref, freq_ref, squares, sems,
                  grad_sems):
    pieces = 4
    rows = grad_ref.shape[0] // pieces
    small = pltpu.make_async_copy(freq_hbm, freq_ref, sems.at[0])
    large = []
    for n in range(pieces):
        here = pl.ds(n * rows, rows)
        large.append(pltpu.make_async_copy(grad_hbm.at[here], grad_ref.at[here], grad_sems.at[n]))
    rest = [
        pltpu.make_async_copy(stacked_hbm, stacked_ref, sems.at[2]),
        pltpu.make_async_copy(mom_hbm, mom_ref, sems.at[3]),
    ]
    for copy in large + [small] + rest:
        copy.start()
    part = jnp.zeros((8, LANES), F32)
    for n, copy in enumerate(large):
        copy.wait()
        g = grad_ref[n * rows:(n + 1) * rows, :].astype(F32)
        g = g * g
        g = g.reshape(-1, 8, g.shape[1]).sum(axis=0)
        part += sum(g[:, m * LANES:(m + 1) * LANES] for m in range(g.shape[1] // LANES))
    part = jnp.sum(part, axis=0, keepdims=True)
    for n in range(squares.shape[0]):
        squares[n] = part
    result = pltpu.make_async_copy(squares, square_hbm, sems.at[1])
    result.start()
    small.wait()
    for col in range(2):
        freq_rows[16 * col:16 * col + 16, :] = jnp.concatenate([freq_ref[:, 4 * col + m, :] for m in range(4)], axis=1)
    result.wait()
    for copy in rest:
        copy.wait()


def table_rows(freqs, stacked):
    places, wide = [], freqs.shape[0] * LANES
    for n in (0, 1):
        index = lax.shift_right_logical(freqs, 6) if n == 0 else lax.bitwise_and(freqs, GROUP - 1)
        places += [index[s:s + 1, :] for s in range(freqs.shape[0])]
    row = lax.broadcasted_iota(jnp.int32, (GROUP, 2 * wide), 0)
    hot = jnp.where(row == jnp.concatenate(places, axis=1), 1.0, 0.0).astype(BF16)
    return dot(stacked, hot).astype(BF16)


def parts(table, s):
    a = slice(s * LANES, (s + 1) * LANES)
    b = slice((s + 8) * LANES, (s + 9) * LANES)
    return table[:GROUP, a], table[GROUP:, a], table[:GROUP, b], table[GROUP:, b]


def diagonal(x):
    lane = lax.broadcasted_iota(jnp.int32, x.shape, 1)
    zero = jnp.zeros_like(x)
    return jnp.concatenate([jnp.where(lane // TOPK == m, x, zero) for m in range(4)], axis=0)


def tile_of(step):
    return pl.multiple_of(step % 2 * TILE[0], TILE[0]), pl.ds(pl.multiple_of(step // 2 * TILE[1], TILE[1]), TILE[1])


def tile_copies(step, pairs, sems):
    top, cols = tile_of(step)
    out = []
    for n, (hbm, tiles, outward) in enumerate(pairs):
        far, near = hbm.at[pl.ds(top, TILE[0]), cols], tiles.at[step]
        out.append(pltpu.make_async_copy(near if outward else far, far if outward else near, sems.at[n, step]))
    return out


def kept_kernel(flag_ref, mom_ref, grad_ref, freq_rows, stacked_ref, out_ref, message_hbm, table, out_sems):
    flag = (flag_ref[0] == 1).astype(F32)
    stacked = stacked_ref[...]
    chunks = freq_rows.shape[0]
    table[0] = table_rows(freq_rows[:8, :], stacked)

    def one(step, carry):
        at = pl.multiple_of(step * 8, 8)
        later = pl.multiple_of(jnp.minimum(step + 1, 3) * 8, 8)
        top, cols = tile_of(step)
        freqs = freq_rows[pl.ds(at, 8), :]
        us, vs = [], []
        for s in range(8):
            rows = pl.ds(top + s * GROUP, GROUP)
            ah, al, bh, bl = parts(table.at[step % 2], s)
            weights = jnp.concatenate([diagonal(bh), diagonal(bl)], axis=1)
            xh, xl = halves(mom_ref[rows, cols])
            y = dot(jnp.concatenate([xh, xl, grad_ref[rows, cols]], axis=0), weights)
            y = y[:, :LANES] + y[:, LANES:]
            a = ah.astype(F32) + al.astype(F32)
            km = jnp.sum((y[:GROUP] + y[GROUP:2 * GROUP]) * a, axis=0, keepdims=True)
            kg = jnp.sum(y[2 * GROUP:] * a, axis=0, keepdims=True)
            us.append(DECAY * km + (1.0 - flag) * kg)
            vs.append(flag * kg)
        table[(step + 1) % 2] = table_rows(freq_rows[pl.ds(later, 8), :], stacked)
        out_ref[pl.ds(at, 8), :] = jnp.concatenate(us, axis=0)
        out_ref[pl.ds(chunks + at, 8), :] = jnp.concatenate(vs, axis=0)
        out_ref[pl.ds(2 * chunks + at, 8), :] = freqs.astype(F32)
        return carry

    lax.fori_loop(0, 4, one, 0)
    copies = [
        pltpu.make_async_copy(out_ref, message_hbm.at[n, pl.ds(0, 3 * chunks)], out_sems.at[n])
        for n in range(message_hbm.shape[0])
    ]
    for copy in copies:
        copy.start()
    for copy in copies:
        copy.wait()


def message_kernel(message_hbm, square_ref, out_hbm, total, sems):
    total[...] = jnp.zeros_like(total)
    total[:1, :] = jnp.sum(square_ref[...], axis=0)
    replicas, rows = out_hbm.shape[:2]
    copies = [pltpu.make_async_copy(total, out_hbm.at[n, pl.ds(rows - 8, 8)], sems.at[n]) for n in range(replicas)]
    for copy in copies:
        copy.start()
    for copy in copies:
        copy.wait()


def own_kernel(flag_ref, mom_hbm, grad_hbm, kept_ref, stacked_ref, u_hbm, v_hbm, mom, grad, u_out, v_out, in_sems, out_sems):
    inward = [(mom_hbm, mom, False), (grad_hbm, grad, False)]
    outward = [(u_hbm, u_out, True), (v_hbm, v_out, True)]
    for step in range(4):
        for copy in tile_copies(step, inward, in_sems):
            copy.start()
    flag = (flag_ref[0] == 1).astype(F32)
    stacked = stacked_ref[...]
    chunks = kept_ref.shape[0] // 3

    def one(step, carry):
        at = pl.multiple_of(step * 8, 8)
        us = kept_ref[pl.ds(at, 8), :]
        vs = kept_ref[pl.ds(chunks + at, 8), :]
        table = table_rows(kept_ref[pl.ds(2 * chunks + at, 8), :].astype(jnp.int32), stacked)
        for copy in tile_copies(step, inward, in_sems):
            copy.wait()
        for s in range(8):
            rows = slice(s * GROUP, (s + 1) * GROUP)
            ah, al, bh, bl = parts(table, s)
            a = ah.astype(F32) + al.astype(F32)
            high, low = halves(jnp.concatenate([a * us[s:s + 1, :], a * vs[s:s + 1, :]], axis=0))
            left = jnp.concatenate([high, low], axis=0)
            right = jnp.concatenate([high, jnp.zeros_like(low)], axis=0)
            y = dot_nt(jnp.concatenate([left, right], axis=1), jnp.concatenate([diagonal(bh), diagonal(bl)], axis=1))
            g = grad[step, rows, :].astype(F32)
            u_out[step, rows, :] = DECAY * mom[step, rows, :] + (1.0 - flag) * g - (y[:GROUP] + y[2 * GROUP:3 * GROUP])
            v_out[step, rows, :] = flag * g - (y[GROUP:2 * GROUP] + y[3 * GROUP:])
        for copy in tile_copies(step, outward, out_sems):
            copy.start()
        return carry

    lax.fori_loop(0, 4, one, 0)
    for step in range(4):
        for copy in tile_copies(step, outward, out_sems):
            copy.wait()


def update_kernel(count, all_ref, u_hbm, v_hbm, rows_ref, cols_ref, mom_hbm, update_hbm, lists_a, lists_b, lists_h, lists_l, pooled, columns,
                  u_ref, v_ref, mom_out, update_out, in_sems, mom_sems, update_sems):
    inward = [(u_hbm, u_ref, False), (v_hbm, v_ref, False)]
    for tile in range(4):
        for copy in tile_copies(tile, inward, in_sems):
            copy.start()
    replicas = all_ref.shape[0]
    chunks = (all_ref.shape[1] - 8) // 3
    total = jnp.sum(all_ref[:, 3 * chunks:, :], axis=0)
    total = jnp.sum(total, axis=(0, 1), keepdims=True)
    rms = jnp.sqrt(total * (1.0 / count))
    factor = jnp.minimum(jnp.float32(1.0), CLIP_RMS / (rms + 1e-06))
    lane = lax.broadcasted_iota(jnp.int32, (8, LANES), 1) // TOPK
    half = TILE[0] // 2

    def regroup(xs, m):
        moved = [x if r == m else pltpu.roll(x, (TOPK * (r - m)) % LANES, 1) for r, x in enumerate(xs)]
        out = moved[0]
        for r in range(1, 4):
            out = jnp.where(lane == r, moved[r], out)
        return out

    def prepare(tile, slot):
        at = pl.multiple_of(tile * 8, 8)
        for group in range(replicas // 4):
            ks, fs = [], []
            for r in range(4 * group, 4 * group + 4):
                u = all_ref[r, pl.ds(at, 8), :]
                v = all_ref[r, pl.ds(chunks + at, 8), :]
                ks.append((u + factor * v) * (1.0 / replicas))
                fs.append(all_ref[r, pl.ds(2 * chunks + at, 8), :])
            for m in range(4):
                k = regroup(ks, m)
                f = regroup(fs, m)
                a = jnp.floor(f * (1.0 / GROUP))
                high = k.astype(BF16).astype(F32)
                place = slice(group * LANES, (group + 1) * LANES)
                lists_a[slot, m, :, place] = a
                lists_b[slot, m, :, place] = f - a * GROUP
                lists_h[slot, m, :, place] = high
                lists_l[slot, m, :, place] = k - high

    items = replicas * TOPK
    place = lax.broadcasted_iota(jnp.int32, (GROUP, items), 0).astype(F32).astype(BF16)
    zero = jnp.zeros((), BF16)

    def scatter(s, m, slot):
        here = slice(s, s + 1)
        a, b, h, l = (x[slot, m, here, :].astype(BF16) for x in (lists_a, lists_b, lists_h, lists_l))
        hit = place == a
        high = jnp.where(hit, h, zero)
        low = jnp.where(hit, l, zero)
        hot = jnp.where(place == b, jnp.ones((), BF16), zero)
        out = dot_nt(jnp.concatenate([high, low], axis=0), hot)
        return out[:GROUP] + out[GROUP:]

    def scatter_row(part, s, slot):
        for pair in range(2):
            both = [scatter(4 * part + s, 2 * pair + n, slot) for n in range(2)]
            pooled[part, s * GROUP:(s + 1) * GROUP, pair * LANES:(pair + 1) * LANES] = jnp.concatenate(both, axis=1)

    def inverse_steps(before, last, out, final=False):
        table_c, table_r = cols_ref[...], rows_ref[...]
        for n in range(2):
            side = slice(n * LANES, (n + 1) * LANES)
            x = dot(table_r, columns[last, n])
            if not final:
                y = dot(jnp.concatenate(halves(pooled[before, :, side]), axis=1), table_c)
            yield
            update_out[out, last, side, :] = x[:LANES] + x[LANES:]
            if final:
                continue
            high, low = halves(y[:, :LANES] + y[:, LANES:])
            for m in range(2):
                here = slice(m * LANES, (m + 1) * LANES)
                columns[before, m, :LANES, side] = high[here]
                columns[before, m, LANES:, side] = low[here]
            yield

    def update_copy(tile, part):
        top, cols = tile_of(tile)
        there = update_hbm.at[pl.ds(top + part * half, half), cols]
        return pltpu.make_async_copy(update_out.at[tile, part], there, update_sems.at[tile, part])

    def mom_copy(tile):
        return tile_copies(tile, [(mom_hbm, mom_out, True)], mom_sems)[0]

    pooled[1] = jnp.zeros(pooled.shape[1:], F32)
    columns[...] = jnp.zeros_like(columns)
    prepare(0, 0)

    def one(tile, carry):
        slot = tile % 2
        before = jnp.maximum(tile - 1, 0)
        prepare(jnp.minimum(tile + 1, 3), 1 - slot)
        for part in range(2):
            for s, unused in enumerate(inverse_steps(1 - part, part, before)):
                scatter_row(part, s, slot)
        for copy in tile_copies(tile, inward, in_sems):
            copy.wait()
        mom_out[tile] = u_ref[tile] + factor * v_ref[tile]
        mom_copy(tile).start()

        @pl.when(tile > 0)
        def _():
            for part in range(2):
                update_copy(before, part).start()

        return carry

    lax.fori_loop(0, 4, one, 0)
    for part in range(2):
        for unused in inverse_steps(1 - part, part, 3, final=part == 1):
            pass
        update_copy(3, part).start()
    for tile in range(4):
        mom_copy(tile).wait()
        for part in range(2):
            update_copy(tile, part).wait()


def spread(copies, axis, minor):
    size = lax.axis_size(axis)
    order = sorted(range(size), key=lambda i: (i % minor, i), reverse=True)
    return lax.all_to_all(copies, axis, 0, 0, axis_index_groups=[order])


def body(momentum, gradient, kept_freq, clip_flag):
    replicas, tensors = lax.axis_size("replica"), lax.axis_size("tensor")
    mom, grad, freq = momentum[0], gradient[0], kept_freq[0]
    rows, cols = mom.shape
    chunks = rows // GROUP * cols // GROUP * TOPK // LANES
    stacked, row_table, col_table = (jnp.asarray(t) for t in tables())
    scalar = pl.BlockSpec(memory_space=pltpu.SMEM)
    hbm = pl.BlockSpec(memory_space=pltpu.HBM)
    vmem = pl.BlockSpec(memory_space=pltpu.VMEM)
    limit = pltpu.CompilerParams(vmem_limit_bytes=32 * 1024 * 1024)
    far = lambda x: pltpu.with_memory_space_constraint(x, pltpu.HBM)
    near = lambda x: pltpu.with_memory_space_constraint(x, pltpu.VMEM)

    squares, grad_near, mom_near, freq_rows, stacked_near = pl.pallas_call(
        square_kernel,
        in_specs=[hbm] * 4,
        out_specs=[hbm] + [vmem] * 4,
        out_shape=[
            pltpu.HBM((tensors, 1, LANES), F32),
            pltpu.VMEM(grad.shape, BF16),
            pltpu.VMEM(mom.shape, F32),
            pltpu.VMEM((chunks, LANES), jnp.int32),
            pltpu.VMEM(stacked.shape, BF16),
        ],
        scratch_shapes=[
            pltpu.VMEM(freq.shape, jnp.int32),
            pltpu.VMEM((tensors, 1, LANES), F32),
            pltpu.SemaphoreType.DMA((4,)),
            pltpu.SemaphoreType.DMA((4,)),
        ],
        compiler_params=limit,
    )(far(grad), far(mom), far(freq), far(stacked))
    squares = spread(squares, "tensor", 2)

    kept, message = pl.pallas_call(
        kept_kernel,
        in_specs=[scalar] + [vmem] * 4,
        out_specs=[vmem, hbm],
        out_shape=[
            pltpu.VMEM((3 * chunks, LANES), F32),
            pltpu.HBM((replicas, 3 * chunks + 8, LANES), F32),
        ],
        scratch_shapes=[
            pltpu.VMEM((2, 2 * GROUP, 16 * LANES), BF16),
            pltpu.SemaphoreType.DMA((replicas,)),
        ],
        compiler_params=limit,
        cost_estimate=pl.CostEstimate(flops=2 * 10 ** 9, bytes_accessed=3 * 2 ** 20, transcendentals=0),
    )(clip_flag, near(mom_near), near(grad_near), near(freq_rows), near(stacked_near))

    message = pl.pallas_call(
        message_kernel,
        in_specs=[hbm, vmem],
        out_specs=hbm,
        out_shape=pltpu.HBM(message.shape, F32),
        input_output_aliases={0: 0},
        scratch_shapes=[pltpu.VMEM((8, LANES), F32), pltpu.SemaphoreType.DMA((replicas,))],
        compiler_params=limit,
    )(far(message), near(squares))
    everyone = spread(message, "replica", 4)

    own_u, own_v = pl.pallas_call(
        own_kernel,
        in_specs=[scalar, hbm, hbm, vmem, vmem],
        out_specs=[hbm] * 2,
        out_shape=[pltpu.HBM((rows, cols), F32)] * 2,
        scratch_shapes=[pltpu.VMEM((4,) + TILE, t) for t in (F32, BF16, F32, F32)] + [pltpu.SemaphoreType.DMA((2, 4))] * 2,
        compiler_params=limit,
        cost_estimate=pl.CostEstimate(flops=2 * 10 ** 9, bytes_accessed=7 * 2 ** 20, transcendentals=0),
    )(clip_flag, far(mom), far(grad), near(kept), near(stacked))

    new_mom, update = pl.pallas_call(
        lambda *refs: update_kernel(replicas * tensors * rows * cols, *refs),
        in_specs=[vmem, hbm, hbm, vmem, vmem],
        out_specs=[hbm] * 2,
        out_shape=[jax.ShapeDtypeStruct((rows, cols), F32)] * 2,
        scratch_shapes=[pltpu.VMEM((2, 4, 8, replicas * TOPK), t) for t in (F32,) * 4]
        + [
            pltpu.VMEM((2, TILE[0] // 2, TILE[1]), F32),
            pltpu.VMEM((2, 2, TILE[0] // 2, TILE[1]), BF16),
            pltpu.VMEM((4,) + TILE, F32),
            pltpu.VMEM((4,) + TILE, F32),
            pltpu.VMEM((4,) + TILE, F32),
            pltpu.VMEM((4, 2, TILE[0] // 2, TILE[1]), F32),
            pltpu.SemaphoreType.DMA((2, 4)),
            pltpu.SemaphoreType.DMA((1, 4)),
            pltpu.SemaphoreType.DMA((4, 2)),
        ],
        compiler_params=limit,
    )(near(everyone), far(own_u), far(own_v), near(row_table), near(col_table))
    return (new_mom[None], update)


def solution(mesh):
    placed = (
        P("replica", None, "tensor"),
        P("replica", None, "tensor"),
        P("replica", None, "tensor", None),
        P("replica"),
    )
    return jax.shard_map(
        body,
        mesh=mesh,
        in_specs=placed,
        out_specs=(P("replica", None, "tensor"), P(None, "tensor")),
        check_vma=False,
    )
```

```python
import math

import jax
import jax.numpy as jnp
import ml_dtypes
import numpy as np
from jax import lax
from jax.experimental import pallas as pl
from jax.experimental.pallas import tpu as pltpu
from jax.sharding import PartitionSpec as P

GROUP = 64
TOPK = 32
LANES = 128
TILE = (512, 256)
CLIP_RMS = 0.5
DECAY = 0.9
F32 = jnp.float32
BF16 = jnp.bfloat16


def split_table(table):
    high = table.astype(ml_dtypes.bfloat16)
    low = (table - high.astype(np.float64)).astype(ml_dtypes.bfloat16)
    return high, low


def tables():
    freq = np.arange(GROUP)[:, None]
    place = np.arange(GROUP)[None, :]
    table = np.sqrt(np.where(freq == 0, 1.0, 2.0) / GROUP) * np.cos(math.pi * (2 * place + 1) * freq / (2 * GROUP))
    high, low = split_table(table)
    stacked = np.concatenate([high.T, low.T], axis=0)
    pair = [np.kron(np.eye(2), t.astype(np.float64)) for t in (high, low)]
    none = np.zeros_like(pair[0])
    cols = np.block([[pair[0], pair[1]], [pair[0], none]]).astype(ml_dtypes.bfloat16)
    rows = np.block([[pair[0].T, pair[0].T], [pair[1].T, none]]).astype(ml_dtypes.bfloat16)
    return stacked, rows, cols


def halves(x):
    high = x.astype(BF16)
    return high, (x - high.astype(F32)).astype(BF16)


def dot(a, b):
    return jnp.dot(a, b, preferred_element_type=F32)


def dot_nt(a, b):
    return lax.dot_general(a, b, (((1,), (1,)), ((), ())), preferred_element_type=F32)


def square_kernel(grad_hbm, mom_hbm, freq_hbm, stacked_hbm, square_hbm, grad_ref, mom_ref, freq_rows, stacked_ref, freq_ref, squares, sems,
                  grad_sems):
    pieces = 4
    rows = grad_ref.shape[0] // pieces
    small = pltpu.make_async_copy(freq_hbm, freq_ref, sems.at[0])
    large = []
    for n in range(pieces):
        here = pl.ds(n * rows, rows)
        large.append(pltpu.make_async_copy(grad_hbm.at[here], grad_ref.at[here], grad_sems.at[n]))
    rest = [
        pltpu.make_async_copy(stacked_hbm, stacked_ref, sems.at[2]),
        pltpu.make_async_copy(mom_hbm, mom_ref, sems.at[3]),
    ]
    for copy in large + [small] + rest:
        copy.start()
    part = jnp.zeros((8, LANES), F32)
    for n, copy in enumerate(large):
        copy.wait()
        g = grad_ref[n * rows:(n + 1) * rows, :].astype(F32)
        g = g * g
        g = g.reshape(-1, 8, g.shape[1]).sum(axis=0)
        part += sum(g[:, m * LANES:(m + 1) * LANES] for m in range(g.shape[1] // LANES))
    part = jnp.sum(part, axis=0, keepdims=True)
    for n in range(squares.shape[0]):
        squares[n] = part
    result = pltpu.make_async_copy(squares, square_hbm, sems.at[1])
    result.start()
    small.wait()
    for col in range(2):
        freq_rows[16 * col:16 * col + 16, :] = jnp.concatenate([freq_ref[:, 4 * col + m, :] for m in range(4)], axis=1)
    result.wait()
    for copy in rest:
        copy.wait()


def table_rows(freqs, stacked):
    places, wide = [], freqs.shape[0] * LANES
    for n in (0, 1):
        index = lax.shift_right_logical(freqs, 6) if n == 0 else lax.bitwise_and(freqs, GROUP - 1)
        places += [index[s:s + 1, :] for s in range(freqs.shape[0])]
    row = lax.broadcasted_iota(jnp.int32, (GROUP, 2 * wide), 0)
    hot = jnp.where(row == jnp.concatenate(places, axis=1), 1.0, 0.0).astype(BF16)
    return dot(stacked, hot).astype(BF16)


def parts(table, s):
    a = slice(s * LANES, (s + 1) * LANES)
    b = slice((s + 8) * LANES, (s + 9) * LANES)
    return table[:GROUP, a], table[GROUP:, a], table[:GROUP, b], table[GROUP:, b]


def diagonal(x):
    lane = lax.broadcasted_iota(jnp.int32, x.shape, 1)
    zero = jnp.zeros_like(x)
    return jnp.concatenate([jnp.where(lane // TOPK == m, x, zero) for m in range(4)], axis=0)


def tile_of(step):
    return pl.multiple_of(step % 2 * TILE[0], TILE[0]), pl.ds(pl.multiple_of(step // 2 * TILE[1], TILE[1]), TILE[1])


def tile_copies(step, pairs, sems):
    top, cols = tile_of(step)
    out = []
    for n, (hbm, tiles, outward) in enumerate(pairs):
        far, near = hbm.at[pl.ds(top, TILE[0]), cols], tiles.at[step]
        out.append(pltpu.make_async_copy(near if outward else far, far if outward else near, sems.at[n, step]))
    return out


def kept_kernel(flag_ref, mom_ref, grad_ref, freq_rows, stacked_ref, out_ref, message_hbm, table, packed, out_sems):
    flag = (flag_ref[0] == 1).astype(F32)
    stacked = stacked_ref[...]
    chunks = freq_rows.shape[0]
    table[0] = table_rows(freq_rows[:8, :], stacked)

    def one(step, carry):
        at = pl.multiple_of(step * 8, 8)
        later = pl.multiple_of(jnp.minimum(step + 1, 3) * 8, 8)
        top, cols = tile_of(step)
        freqs = freq_rows[pl.ds(at, 8), :]
        us, vs = [], []
        for s in range(8):
            rows = pl.ds(top + s * GROUP, GROUP)
            ah, al, bh, bl = parts(table.at[step % 2], s)
            weights = jnp.concatenate([diagonal(bh), diagonal(bl)], axis=1)
            xh, xl = halves(mom_ref[rows, cols])
            y = dot(jnp.concatenate([xh, xl, grad_ref[rows, cols]], axis=0), weights)
            y = y[:, :LANES] + y[:, LANES:]
            a = ah.astype(F32) + al.astype(F32)
            km = jnp.sum((y[:GROUP] + y[GROUP:2 * GROUP]) * a, axis=0, keepdims=True)
            kg = jnp.sum(y[2 * GROUP:] * a, axis=0, keepdims=True)
            us.append(DECAY * km + (1.0 - flag) * kg)
            vs.append(flag * kg)
        table[(step + 1) % 2] = table_rows(freq_rows[pl.ds(later, 8), :], stacked)
        out_ref[pl.ds(at, 8), :] = jnp.concatenate(us, axis=0)
        out_ref[pl.ds(chunks + at, 8), :] = jnp.concatenate(vs, axis=0)
        out_ref[pl.ds(2 * chunks + at, 8), :] = freqs.astype(F32)
        return carry

    lax.fori_loop(0, 4, one, 0)
    packed[:, 0, :] = out_ref[...]
    copies = [
        pltpu.make_async_copy(packed, message_hbm.at[n, pl.ds(0, 3 * chunks)], out_sems.at[n])
        for n in range(message_hbm.shape[0])
    ]
    for copy in copies:
        copy.start()
    for copy in copies:
        copy.wait()


def message_kernel(message_hbm, square_ref, out_hbm, total, sems):
    total[...] = jnp.sum(square_ref[...], axis=0, keepdims=True)
    replicas, rows = out_hbm.shape[:2]
    copies = [pltpu.make_async_copy(total, out_hbm.at[n, pl.ds(rows - 1, 1)], sems.at[n]) for n in range(replicas)]
    for copy in copies:
        copy.start()
    for copy in copies:
        copy.wait()


def own_kernel(flag_ref, mom_hbm, grad_hbm, kept_ref, stacked_ref, u_hbm, v_hbm, mom, grad, u_out, v_out, in_sems, out_sems):
    inward = [(mom_hbm, mom, False), (grad_hbm, grad, False)]
    outward = [(u_hbm, u_out, True), (v_hbm, v_out, True)]
    for step in range(4):
        for copy in tile_copies(step, inward, in_sems):
            copy.start()
    flag = (flag_ref[0] == 1).astype(F32)
    stacked = stacked_ref[...]
    chunks = kept_ref.shape[0] // 3

    def one(step, carry):
        at = pl.multiple_of(step * 8, 8)
        us = kept_ref[pl.ds(at, 8), :]
        vs = kept_ref[pl.ds(chunks + at, 8), :]
        table = table_rows(kept_ref[pl.ds(2 * chunks + at, 8), :].astype(jnp.int32), stacked)
        for copy in tile_copies(step, inward, in_sems):
            copy.wait()
        for s in range(8):
            rows = slice(s * GROUP, (s + 1) * GROUP)
            ah, al, bh, bl = parts(table, s)
            a = ah.astype(F32) + al.astype(F32)
            high, low = halves(jnp.concatenate([a * us[s:s + 1, :], a * vs[s:s + 1, :]], axis=0))
            left = jnp.concatenate([high, low], axis=0)
            right = jnp.concatenate([high, jnp.zeros_like(low)], axis=0)
            y = dot_nt(jnp.concatenate([left, right], axis=1), jnp.concatenate([diagonal(bh), diagonal(bl)], axis=1))
            g = grad[step, rows, :].astype(F32)
            u_out[step, rows, :] = DECAY * mom[step, rows, :] + (1.0 - flag) * g - (y[:GROUP] + y[2 * GROUP:3 * GROUP])
            v_out[step, rows, :] = flag * g - (y[GROUP:2 * GROUP] + y[3 * GROUP:])
        for copy in tile_copies(step, outward, out_sems):
            copy.start()
        return carry

    lax.fori_loop(0, 4, one, 0)
    for step in range(4):
        for copy in tile_copies(step, outward, out_sems):
            copy.wait()


def update_kernel(count, all_ref, u_hbm, v_hbm, rows_ref, cols_ref, mom_hbm, update_hbm, lists_a, lists_b, lists_h, lists_l, pooled, columns,
                  u_ref, v_ref, mom_out, update_out, in_sems, mom_sems, update_sems):
    inward = [(u_hbm, u_ref, False), (v_hbm, v_ref, False)]
    for tile in range(4):
        for copy in tile_copies(tile, inward, in_sems):
            copy.start()
    replicas = all_ref.shape[0]
    chunks = (all_ref.shape[1] - 1) // 3
    total = jnp.sum(all_ref[:, 3 * chunks, 0, :], axis=(0, 1), keepdims=True)
    rms = jnp.sqrt(total * (1.0 / count))
    factor = jnp.minimum(jnp.float32(1.0), CLIP_RMS / (rms + 1e-06))
    lane = lax.broadcasted_iota(jnp.int32, (8, LANES), 1) // TOPK
    half = TILE[0] // 2

    def regroup(xs, m):
        moved = [x if r == m else pltpu.roll(x, (TOPK * (r - m)) % LANES, 1) for r, x in enumerate(xs)]
        out = moved[0]
        for r in range(1, 4):
            out = jnp.where(lane == r, moved[r], out)
        return out

    def prepare(tile, slot):
        at = pl.multiple_of(tile * 8, 8)
        for group in range(replicas // 4):
            ks, fs = [], []
            for r in range(4 * group, 4 * group + 4):
                u = all_ref[r, pl.ds(at, 8), 0, :]
                v = all_ref[r, pl.ds(chunks + at, 8), 0, :]
                ks.append((u + factor * v) * (1.0 / replicas))
                fs.append(all_ref[r, pl.ds(2 * chunks + at, 8), 0, :])
            for m in range(4):
                k = regroup(ks, m)
                f = regroup(fs, m)
                a = jnp.floor(f * (1.0 / GROUP))
                high = k.astype(BF16).astype(F32)
                place = slice(group * LANES, (group + 1) * LANES)
                lists_a[slot, m, :, place] = a
                lists_b[slot, m, :, place] = f - a * GROUP
                lists_h[slot, m, :, place] = high
                lists_l[slot, m, :, place] = k - high

    items = replicas * TOPK
    place = lax.broadcasted_iota(jnp.int32, (GROUP, items), 0).astype(F32).astype(BF16)
    zero = jnp.zeros((), BF16)

    def scatter(s, m, slot):
        here = slice(s, s + 1)
        a, b, h, l = (x[slot, m, here, :].astype(BF16) for x in (lists_a, lists_b, lists_h, lists_l))
        hit = place == a
        high = jnp.where(hit, h, zero)
        low = jnp.where(hit, l, zero)
        hot = jnp.where(place == b, jnp.ones((), BF16), zero)
        out = dot_nt(jnp.concatenate([high, low], axis=0), hot)
        return out[:GROUP] + out[GROUP:]

    def scatter_row(part, s, slot):
        for pair in range(2):
            both = [scatter(4 * part + s, 2 * pair + n, slot) for n in range(2)]
            pooled[part, s * GROUP:(s + 1) * GROUP, pair * LANES:(pair + 1) * LANES] = jnp.concatenate(both, axis=1)

    def inverse_steps(before, last, out, final=False):
        table_c, table_r = cols_ref[...], rows_ref[...]
        for n in range(2):
            side = slice(n * LANES, (n + 1) * LANES)
            x = dot(table_r, columns[last, n])
            if not final:
                y = dot(jnp.concatenate(halves(pooled[before, :, side]), axis=1), table_c)
            yield
            update_out[out, last, side, :] = x[:LANES] + x[LANES:]
            if final:
                continue
            high, low = halves(y[:, :LANES] + y[:, LANES:])
            for m in range(2):
                here = slice(m * LANES, (m + 1) * LANES)
                columns[before, m, :LANES, side] = high[here]
                columns[before, m, LANES:, side] = low[here]
            yield

    def update_copy(tile, part):
        top, cols = tile_of(tile)
        there = update_hbm.at[pl.ds(top + part * half, half), cols]
        return pltpu.make_async_copy(update_out.at[tile, part], there, update_sems.at[tile, part])

    def mom_copy(tile):
        return tile_copies(tile, [(mom_hbm, mom_out, True)], mom_sems)[0]

    pooled[1] = jnp.zeros(pooled.shape[1:], F32)
    columns[...] = jnp.zeros_like(columns)
    prepare(0, 0)

    def one(tile, carry):
        slot = tile % 2
        before = jnp.maximum(tile - 1, 0)
        prepare(jnp.minimum(tile + 1, 3), 1 - slot)
        for part in range(2):
            for s, unused in enumerate(inverse_steps(1 - part, part, before)):
                scatter_row(part, s, slot)
        for copy in tile_copies(tile, inward, in_sems):
            copy.wait()
        mom_out[tile] = u_ref[tile] + factor * v_ref[tile]
        mom_copy(tile).start()

        @pl.when(tile > 0)
        def _():
            for part in range(2):
                update_copy(before, part).start()

        return carry

    lax.fori_loop(0, 4, one, 0)
    for part in range(2):
        for unused in inverse_steps(1 - part, part, 3, final=part == 1):
            pass
        update_copy(3, part).start()
    for tile in range(4):
        mom_copy(tile).wait()
        for part in range(2):
            update_copy(tile, part).wait()


def spread(copies, axis, minor):
    size = lax.axis_size(axis)
    order = sorted(range(size), key=lambda i: (i % minor, i), reverse=True)
    return lax.all_to_all(copies, axis, 0, 0, axis_index_groups=[order])


def body(momentum, gradient, kept_freq, clip_flag):
    replicas, tensors = lax.axis_size("replica"), lax.axis_size("tensor")
    mom, grad, freq = momentum[0], gradient[0], kept_freq[0]
    rows, cols = mom.shape
    chunks = rows // GROUP * cols // GROUP * TOPK // LANES
    stacked, row_table, col_table = (jnp.asarray(t) for t in tables())
    scalar = pl.BlockSpec(memory_space=pltpu.SMEM)
    hbm = pl.BlockSpec(memory_space=pltpu.HBM)
    vmem = pl.BlockSpec(memory_space=pltpu.VMEM)
    limit = pltpu.CompilerParams(vmem_limit_bytes=32 * 1024 * 1024)
    far = lambda x: pltpu.with_memory_space_constraint(x, pltpu.HBM)
    near = lambda x: pltpu.with_memory_space_constraint(x, pltpu.VMEM)

    squares, grad_near, mom_near, freq_rows, stacked_near = pl.pallas_call(
        square_kernel,
        in_specs=[hbm] * 4,
        out_specs=[hbm] + [vmem] * 4,
        out_shape=[
            pltpu.HBM((tensors, 1, LANES), F32),
            pltpu.VMEM(grad.shape, BF16),
            pltpu.VMEM(mom.shape, F32),
            pltpu.VMEM((chunks, LANES), jnp.int32),
            pltpu.VMEM(stacked.shape, BF16),
        ],
        scratch_shapes=[
            pltpu.VMEM(freq.shape, jnp.int32),
            pltpu.VMEM((tensors, 1, LANES), F32),
            pltpu.SemaphoreType.DMA((4,)),
            pltpu.SemaphoreType.DMA((4,)),
        ],
        compiler_params=limit,
    )(far(grad), far(mom), far(freq), far(stacked))
    squares = spread(squares, "tensor", 2)

    kept, message = pl.pallas_call(
        kept_kernel,
        in_specs=[scalar] + [vmem] * 4,
        out_specs=[vmem, hbm],
        out_shape=[
            pltpu.VMEM((3 * chunks, LANES), F32),
            pltpu.HBM((replicas, 3 * chunks + 1, 1, LANES), F32),
        ],
        scratch_shapes=[
            pltpu.VMEM((2, 2 * GROUP, 16 * LANES), BF16),
            pltpu.VMEM((3 * chunks, 1, LANES), F32),
            pltpu.SemaphoreType.DMA((replicas,)),
        ],
        compiler_params=limit,
        cost_estimate=pl.CostEstimate(flops=2 * 10 ** 9, bytes_accessed=3 * 2 ** 20, transcendentals=0),
    )(clip_flag, near(mom_near), near(grad_near), near(freq_rows), near(stacked_near))

    message = pl.pallas_call(
        message_kernel,
        in_specs=[hbm, vmem],
        out_specs=hbm,
        out_shape=pltpu.HBM(message.shape, F32),
        input_output_aliases={0: 0},
        scratch_shapes=[pltpu.VMEM((1, 1, LANES), F32), pltpu.SemaphoreType.DMA((replicas,))],
        compiler_params=limit,
    )(far(message), near(squares))
    everyone = spread(message, "replica", 4)

    own_u, own_v = pl.pallas_call(
        own_kernel,
        in_specs=[scalar, hbm, hbm, vmem, vmem],
        out_specs=[hbm] * 2,
        out_shape=[pltpu.HBM((rows, cols), F32)] * 2,
        scratch_shapes=[pltpu.VMEM((4,) + TILE, t) for t in (F32, BF16, F32, F32)] + [pltpu.SemaphoreType.DMA((2, 4))] * 2,
        compiler_params=limit,
        cost_estimate=pl.CostEstimate(flops=2 * 10 ** 9, bytes_accessed=7 * 2 ** 20, transcendentals=0),
    )(clip_flag, far(mom), far(grad), near(kept), near(stacked))

    new_mom, update = pl.pallas_call(
        lambda *refs: update_kernel(replicas * tensors * rows * cols, *refs),
        in_specs=[vmem, hbm, hbm, vmem, vmem],
        out_specs=[hbm] * 2,
        out_shape=[jax.ShapeDtypeStruct((rows, cols), F32)] * 2,
        scratch_shapes=[pltpu.VMEM((2, 4, 8, replicas * TOPK), t) for t in (F32,) * 4]
        + [
            pltpu.VMEM((2, TILE[0] // 2, TILE[1]), F32),
            pltpu.VMEM((2, 2, TILE[0] // 2, TILE[1]), BF16),
            pltpu.VMEM((4,) + TILE, F32),
            pltpu.VMEM((4,) + TILE, F32),
            pltpu.VMEM((4,) + TILE, F32),
            pltpu.VMEM((4, 2, TILE[0] // 2, TILE[1]), F32),
            pltpu.SemaphoreType.DMA((2, 4)),
            pltpu.SemaphoreType.DMA((1, 4)),
            pltpu.SemaphoreType.DMA((4, 2)),
        ],
        compiler_params=limit,
    )(near(everyone), far(own_u), far(own_v), near(row_table), near(col_table))
    return (new_mom[None], update)


def solution(mesh):
    placed = (
        P("replica", None, "tensor"),
        P("replica", None, "tensor"),
        P("replica", None, "tensor", None),
        P("replica"),
    )
    return jax.shard_map(
        body,
        mesh=mesh,
        in_specs=placed,
        out_specs=(P("replica", None, "tensor"), P(None, "tensor")),
        check_vma=False,
    )
```

```python
import math

import jax
import jax.numpy as jnp
import ml_dtypes
import numpy as np
from jax import lax
from jax.experimental import pallas as pl
from jax.experimental.pallas import tpu as pltpu
from jax.sharding import PartitionSpec as P

GROUP = 64
TOPK = 32
LANES = 128
TILE = (512, 256)
CLIP_RMS = 0.5
DECAY = 0.9
F32 = jnp.float32
BF16 = jnp.bfloat16


def split_table(table):
    high = table.astype(ml_dtypes.bfloat16)
    low = (table - high.astype(np.float64)).astype(ml_dtypes.bfloat16)
    return high, low


def tables():
    freq = np.arange(GROUP)[:, None]
    place = np.arange(GROUP)[None, :]
    table = np.sqrt(np.where(freq == 0, 1.0, 2.0) / GROUP) * np.cos(math.pi * (2 * place + 1) * freq / (2 * GROUP))
    high, low = split_table(table)
    stacked = np.concatenate([high.T, low.T], axis=0)
    pair = [np.kron(np.eye(2), t.astype(np.float64)) for t in (high, low)]
    none = np.zeros_like(pair[0])
    cols = np.block([[pair[0], pair[1]], [pair[0], none]]).astype(ml_dtypes.bfloat16)
    rows = np.block([[pair[0].T, pair[0].T], [pair[1].T, none]]).astype(ml_dtypes.bfloat16)
    return stacked, rows, cols


def halves(x):
    high = x.astype(BF16)
    return high, (x - high.astype(F32)).astype(BF16)


def dot(a, b):
    return jnp.dot(a, b, preferred_element_type=F32)


def dot_nt(a, b):
    return lax.dot_general(a, b, (((1,), (1,)), ((), ())), preferred_element_type=F32)


def square_kernel(grad_hbm, mom_hbm, freq_hbm, stacked_hbm, square_hbm, grad_ref, mom_ref, freq_rows, stacked_ref, freq_ref, squares, sems,
                  grad_sems):
    pieces = 4
    rows = grad_ref.shape[0] // pieces
    small = pltpu.make_async_copy(freq_hbm, freq_ref, sems.at[0])
    large = []
    for n in range(pieces):
        here = pl.ds(n * rows, rows)
        large.append(pltpu.make_async_copy(grad_hbm.at[here], grad_ref.at[here], grad_sems.at[n]))
    rest = [
        pltpu.make_async_copy(stacked_hbm, stacked_ref, sems.at[2]),
        pltpu.make_async_copy(mom_hbm, mom_ref, sems.at[3]),
    ]
    for copy in large + [small] + rest:
        copy.start()
    part = jnp.zeros((8, LANES), F32)
    for n, copy in enumerate(large):
        copy.wait()
        g = grad_ref[n * rows:(n + 1) * rows, :].astype(F32)
        g = g * g
        g = g.reshape(-1, 8, g.shape[1]).sum(axis=0)
        part += sum(g[:, m * LANES:(m + 1) * LANES] for m in range(g.shape[1] // LANES))
    part = jnp.sum(part, axis=0, keepdims=True)
    for n in range(squares.shape[0]):
        squares[n] = part
    result = pltpu.make_async_copy(squares, square_hbm, sems.at[1])
    result.start()
    small.wait()
    for col in range(2):
        freq_rows[16 * col:16 * col + 16, :] = jnp.concatenate([freq_ref[:, 4 * col + m, :] for m in range(4)], axis=1)
    result.wait()
    for copy in rest:
        copy.wait()


def table_rows(freqs, stacked):
    places, wide = [], freqs.shape[0] * LANES
    for n in (0, 1):
        index = lax.shift_right_logical(freqs, 6) if n == 0 else lax.bitwise_and(freqs, GROUP - 1)
        places += [index[s:s + 1, :] for s in range(freqs.shape[0])]
    row = lax.broadcasted_iota(jnp.int32, (GROUP, 2 * wide), 0)
    hot = jnp.where(row == jnp.concatenate(places, axis=1), 1.0, 0.0).astype(BF16)
    return dot(stacked, hot).astype(BF16)


def parts(table, s):
    a = slice(s * LANES, (s + 1) * LANES)
    b = slice((s + 8) * LANES, (s + 9) * LANES)
    return table[:GROUP, a], table[GROUP:, a], table[:GROUP, b], table[GROUP:, b]


def diagonal(x):
    lane = lax.broadcasted_iota(jnp.int32, x.shape, 1)
    zero = jnp.zeros_like(x)
    return jnp.concatenate([jnp.where(lane // TOPK == m, x, zero) for m in range(4)], axis=0)


def tile_of(step):
    return pl.multiple_of(step % 2 * TILE[0], TILE[0]), pl.ds(pl.multiple_of(step // 2 * TILE[1], TILE[1]), TILE[1])


def tile_copies(step, pairs, sems):
    top, cols = tile_of(step)
    out = []
    for n, (hbm, tiles, outward) in enumerate(pairs):
        far, near = hbm.at[pl.ds(top, TILE[0]), cols], tiles.at[step]
        out.append(pltpu.make_async_copy(near if outward else far, far if outward else near, sems.at[n, step]))
    return out


def kept_kernel(flag_ref, mom_ref, grad_ref, freq_rows, stacked_ref, out_ref, message_hbm, table, packed, out_sems):
    flag = (flag_ref[0] == 1).astype(F32)
    stacked = stacked_ref[...]
    chunks = freq_rows.shape[0]
    table[0] = table_rows(freq_rows[:8, :], stacked)

    def one(step, carry):
        at = pl.multiple_of(step * 8, 8)
        later = pl.multiple_of(jnp.minimum(step + 1, 3) * 8, 8)
        top, cols = tile_of(step)
        freqs = freq_rows[pl.ds(at, 8), :]
        us, vs = [], []
        for s in range(8):
            rows = pl.ds(top + s * GROUP, GROUP)
            ah, al, bh, bl = parts(table.at[step % 2], s)
            weights = jnp.concatenate([diagonal(bh), diagonal(bl)], axis=1)
            xh, xl = halves(mom_ref[rows, cols])
            y = dot(jnp.concatenate([xh, xl, grad_ref[rows, cols]], axis=0), weights)
            y = y[:, :LANES] + y[:, LANES:]
            a = ah.astype(F32) + al.astype(F32)
            km = jnp.sum((y[:GROUP] + y[GROUP:2 * GROUP]) * a, axis=0, keepdims=True)
            kg = jnp.sum(y[2 * GROUP:] * a, axis=0, keepdims=True)
            us.append(DECAY * km + (1.0 - flag) * kg)
            vs.append(flag * kg)
        table[(step + 1) % 2] = table_rows(freq_rows[pl.ds(later, 8), :], stacked)
        out_ref[pl.ds(at, 8), :] = jnp.concatenate(us, axis=0)
        out_ref[pl.ds(chunks + at, 8), :] = jnp.concatenate(vs, axis=0)
        out_ref[pl.ds(2 * chunks + at, 8), :] = freqs.astype(F32)
        return carry

    lax.fori_loop(0, 4, one, 0)
    packed[:, 0, :] = out_ref[...]
    copies = [
        pltpu.make_async_copy(packed, message_hbm.at[n, pl.ds(0, 3 * chunks)], out_sems.at[n])
        for n in range(message_hbm.shape[0])
    ]
    for copy in copies:
        copy.start()
    for copy in copies:
        copy.wait()


def message_kernel(message_hbm, square_ref, out_hbm, total, sem):
    replicas, rows = out_hbm.shape[:2]
    line = jnp.sum(square_ref[...], axis=0, keepdims=True)
    for n in range(replicas):
        total[n] = line
    copy = pltpu.make_async_copy(total, out_hbm.at[:, pl.ds(rows - 1, 1)], sem)
    copy.start()
    copy.wait()


def own_kernel(flag_ref, mom_hbm, grad_hbm, kept_ref, stacked_ref, u_hbm, v_hbm, mom, grad, u_out, v_out, in_sems, out_sems):
    inward = [(mom_hbm, mom, False), (grad_hbm, grad, False)]
    outward = [(u_hbm, u_out, True), (v_hbm, v_out, True)]
    for step in range(4):
        for copy in tile_copies(step, inward, in_sems):
            copy.start()
    flag = (flag_ref[0] == 1).astype(F32)
    stacked = stacked_ref[...]
    chunks = kept_ref.shape[0] // 3

    def one(step, carry):
        at = pl.multiple_of(step * 8, 8)
        us = kept_ref[pl.ds(at, 8), :]
        vs = kept_ref[pl.ds(chunks + at, 8), :]
        table = table_rows(kept_ref[pl.ds(2 * chunks + at, 8), :].astype(jnp.int32), stacked)
        for copy in tile_copies(step, inward, in_sems):
            copy.wait()
        for s in range(8):
            rows = slice(s * GROUP, (s + 1) * GROUP)
            ah, al, bh, bl = parts(table, s)
            a = ah.astype(F32) + al.astype(F32)
            high, low = halves(jnp.concatenate([a * us[s:s + 1, :], a * vs[s:s + 1, :]], axis=0))
            left = jnp.concatenate([high, low], axis=0)
            right = jnp.concatenate([high, jnp.zeros_like(low)], axis=0)
            y = dot_nt(jnp.concatenate([left, right], axis=1), jnp.concatenate([diagonal(bh), diagonal(bl)], axis=1))
            g = grad[step, rows, :].astype(F32)
            u_out[step, rows, :] = DECAY * mom[step, rows, :] + (1.0 - flag) * g - (y[:GROUP] + y[2 * GROUP:3 * GROUP])
            v_out[step, rows, :] = flag * g - (y[GROUP:2 * GROUP] + y[3 * GROUP:])
        for copy in tile_copies(step, outward, out_sems):
            copy.start()
        return carry

    lax.fori_loop(0, 4, one, 0)
    for step in range(4):
        for copy in tile_copies(step, outward, out_sems):
            copy.wait()


def update_kernel(count, all_ref, u_hbm, v_hbm, rows_ref, cols_ref, mom_hbm, update_hbm, lists_a, lists_b, lists_h, lists_l, pooled, columns,
                  u_ref, v_ref, mom_out, update_out, in_sems, mom_sems, update_sems):
    inward = [(u_hbm, u_ref, False), (v_hbm, v_ref, False)]
    for tile in range(4):
        for copy in tile_copies(tile, inward, in_sems):
            copy.start()
    replicas = all_ref.shape[0]
    chunks = (all_ref.shape[1] - 1) // 3
    total = jnp.sum(all_ref[:, 3 * chunks, 0, :], axis=(0, 1), keepdims=True)
    rms = jnp.sqrt(total * (1.0 / count))
    factor = jnp.minimum(jnp.float32(1.0), CLIP_RMS / (rms + 1e-06))
    lane = lax.broadcasted_iota(jnp.int32, (8, LANES), 1) // TOPK
    half = TILE[0] // 2

    def regroup(xs, m):
        moved = [x if r == m else pltpu.roll(x, (TOPK * (r - m)) % LANES, 1) for r, x in enumerate(xs)]
        out = moved[0]
        for r in range(1, 4):
            out = jnp.where(lane == r, moved[r], out)
        return out

    def prepare(tile, slot):
        at = pl.multiple_of(tile * 8, 8)
        for group in range(replicas // 4):
            ks, fs = [], []
            for r in range(4 * group, 4 * group + 4):
                u = all_ref[r, pl.ds(at, 8), 0, :]
                v = all_ref[r, pl.ds(chunks + at, 8), 0, :]
                ks.append((u + factor * v) * (1.0 / replicas))
                fs.append(all_ref[r, pl.ds(2 * chunks + at, 8), 0, :])
            for m in range(4):
                k = regroup(ks, m)
                f = regroup(fs, m)
                a = jnp.floor(f * (1.0 / GROUP))
                high = k.astype(BF16).astype(F32)
                place = slice(group * LANES, (group + 1) * LANES)
                lists_a[slot, m, :, place] = a
                lists_b[slot, m, :, place] = f - a * GROUP
                lists_h[slot, m, :, place] = high
                lists_l[slot, m, :, place] = k - high

    items = replicas * TOPK
    place = lax.broadcasted_iota(jnp.int32, (GROUP, items), 0).astype(F32).astype(BF16)
    zero = jnp.zeros((), BF16)

    def scatter(s, m, slot):
        here = slice(s, s + 1)
        a, b, h, l = (x[slot, m, here, :].astype(BF16) for x in (lists_a, lists_b, lists_h, lists_l))
        hit = place == a
        high = jnp.where(hit, h, zero)
        low = jnp.where(hit, l, zero)
        hot = jnp.where(place == b, jnp.ones((), BF16), zero)
        out = dot_nt(jnp.concatenate([high, low], axis=0), hot)
        return out[:GROUP] + out[GROUP:]

    def scatter_row(part, s, slot):
        for pair in range(2):
            both = [scatter(4 * part + s, 2 * pair + n, slot) for n in range(2)]
            pooled[part, s * GROUP:(s + 1) * GROUP, pair * LANES:(pair + 1) * LANES] = jnp.concatenate(both, axis=1)

    def inverse_steps(before, last, out, final=False):
        table_c, table_r = cols_ref[...], rows_ref[...]
        for n in range(2):
            side = slice(n * LANES, (n + 1) * LANES)
            x = dot(table_r, columns[last, n])
            if not final:
                y = dot(jnp.concatenate(halves(pooled[before, :, side]), axis=1), table_c)
            yield
            update_out[out, last, side, :] = x[:LANES] + x[LANES:]
            if final:
                continue
            high, low = halves(y[:, :LANES] + y[:, LANES:])
            for m in range(2):
                here = slice(m * LANES, (m + 1) * LANES)
                columns[before, m, :LANES, side] = high[here]
                columns[before, m, LANES:, side] = low[here]
            yield

    def update_copy(tile, part):
        top, cols = tile_of(tile)
        there = update_hbm.at[pl.ds(top + part * half, half), cols]
        return pltpu.make_async_copy(update_out.at[tile, part], there, update_sems.at[tile, part])

    def mom_copy(tile):
        return tile_copies(tile, [(mom_hbm, mom_out, True)], mom_sems)[0]

    pooled[1] = jnp.zeros(pooled.shape[1:], F32)
    columns[...] = jnp.zeros_like(columns)
    prepare(0, 0)

    def one(tile, carry):
        slot = tile % 2
        before = jnp.maximum(tile - 1, 0)
        prepare(jnp.minimum(tile + 1, 3), 1 - slot)
        for part in range(2):
            for s, unused in enumerate(inverse_steps(1 - part, part, before)):
                scatter_row(part, s, slot)
        for copy in tile_copies(tile, inward, in_sems):
            copy.wait()
        mom_out[tile] = u_ref[tile] + factor * v_ref[tile]
        mom_copy(tile).start()

        @pl.when(tile > 0)
        def _():
            for part in range(2):
                update_copy(before, part).start()

        return carry

    lax.fori_loop(0, 4, one, 0)
    for part in range(2):
        for unused in inverse_steps(1 - part, part, 3, final=part == 1):
            pass
        update_copy(3, part).start()
    for tile in range(4):
        mom_copy(tile).wait()
        for part in range(2):
            update_copy(tile, part).wait()


def spread(copies, axis, minor):
    size = lax.axis_size(axis)
    order = sorted(range(size), key=lambda i: (i % minor, i), reverse=True)
    return lax.all_to_all(copies, axis, 0, 0, axis_index_groups=[order])


def body(momentum, gradient, kept_freq, clip_flag):
    replicas, tensors = lax.axis_size("replica"), lax.axis_size("tensor")
    mom, grad, freq = momentum[0], gradient[0], kept_freq[0]
    rows, cols = mom.shape
    chunks = rows // GROUP * cols // GROUP * TOPK // LANES
    stacked, row_table, col_table = (jnp.asarray(t) for t in tables())
    scalar = pl.BlockSpec(memory_space=pltpu.SMEM)
    hbm = pl.BlockSpec(memory_space=pltpu.HBM)
    vmem = pl.BlockSpec(memory_space=pltpu.VMEM)
    limit = pltpu.CompilerParams(vmem_limit_bytes=32 * 1024 * 1024)
    far = lambda x: pltpu.with_memory_space_constraint(x, pltpu.HBM)
    near = lambda x: pltpu.with_memory_space_constraint(x, pltpu.VMEM)

    squares, grad_near, mom_near, freq_rows, stacked_near = pl.pallas_call(
        square_kernel,
        in_specs=[hbm] * 4,
        out_specs=[hbm] + [vmem] * 4,
        out_shape=[
            pltpu.HBM((tensors, 1, LANES), F32),
            pltpu.VMEM(grad.shape, BF16),
            pltpu.VMEM(mom.shape, F32),
            pltpu.VMEM((chunks, LANES), jnp.int32),
            pltpu.VMEM(stacked.shape, BF16),
        ],
        scratch_shapes=[
            pltpu.VMEM(freq.shape, jnp.int32),
            pltpu.VMEM((tensors, 1, LANES), F32),
            pltpu.SemaphoreType.DMA((4,)),
            pltpu.SemaphoreType.DMA((4,)),
        ],
        compiler_params=limit,
    )(far(grad), far(mom), far(freq), far(stacked))
    squares = spread(squares, "tensor", 2)

    kept, message = pl.pallas_call(
        kept_kernel,
        in_specs=[scalar] + [vmem] * 4,
        out_specs=[vmem, hbm],
        out_shape=[
            pltpu.VMEM((3 * chunks, LANES), F32),
            pltpu.HBM((replicas, 3 * chunks + 1, 1, LANES), F32),
        ],
        scratch_shapes=[
            pltpu.VMEM((2, 2 * GROUP, 16 * LANES), BF16),
            pltpu.VMEM((3 * chunks, 1, LANES), F32),
            pltpu.SemaphoreType.DMA((replicas,)),
        ],
        compiler_params=limit,
        cost_estimate=pl.CostEstimate(flops=2 * 10 ** 9, bytes_accessed=3 * 2 ** 20, transcendentals=0),
    )(clip_flag, near(mom_near), near(grad_near), near(freq_rows), near(stacked_near))

    message = pl.pallas_call(
        message_kernel,
        in_specs=[hbm, vmem],
        out_specs=hbm,
        out_shape=pltpu.HBM(message.shape, F32),
        input_output_aliases={0: 0},
        scratch_shapes=[pltpu.VMEM((replicas, 1, 1, LANES), F32), pltpu.SemaphoreType.DMA],
        compiler_params=limit,
    )(far(message), near(squares))
    everyone = spread(message, "replica", 4)

    own_u, own_v = pl.pallas_call(
        own_kernel,
        in_specs=[scalar, hbm, hbm, vmem, vmem],
        out_specs=[hbm] * 2,
        out_shape=[pltpu.HBM((rows, cols), F32)] * 2,
        scratch_shapes=[pltpu.VMEM((4,) + TILE, t) for t in (F32, BF16, F32, F32)] + [pltpu.SemaphoreType.DMA((2, 4))] * 2,
        compiler_params=limit,
        cost_estimate=pl.CostEstimate(flops=2 * 10 ** 9, bytes_accessed=7 * 2 ** 20, transcendentals=0),
    )(clip_flag, far(mom), far(grad), near(kept), near(stacked))

    new_mom, update = pl.pallas_call(
        lambda *refs: update_kernel(replicas * tensors * rows * cols, *refs),
        in_specs=[vmem, hbm, hbm, vmem, vmem],
        out_specs=[hbm] * 2,
        out_shape=[jax.ShapeDtypeStruct((rows, cols), F32)] * 2,
        scratch_shapes=[pltpu.VMEM((2, 4, 8, replicas * TOPK), t) for t in (F32,) * 4]
        + [
            pltpu.VMEM((2, TILE[0] // 2, TILE[1]), F32),
            pltpu.VMEM((2, 2, TILE[0] // 2, TILE[1]), BF16),
            pltpu.VMEM((4,) + TILE, F32),
            pltpu.VMEM((4,) + TILE, F32),
            pltpu.VMEM((4,) + TILE, F32),
            pltpu.VMEM((4, 2, TILE[0] // 2, TILE[1]), F32),
            pltpu.SemaphoreType.DMA((2, 4)),
            pltpu.SemaphoreType.DMA((1, 4)),
            pltpu.SemaphoreType.DMA((4, 2)),
        ],
        compiler_params=limit,
    )(near(everyone), far(own_u), far(own_v), near(row_table), near(col_table))
    return (new_mom[None], update)


def solution(mesh):
    placed = (
        P("replica", None, "tensor"),
        P("replica", None, "tensor"),
        P("replica", None, "tensor", None),
        P("replica"),
    )
    return jax.shard_map(
        body,
        mesh=mesh,
        in_specs=placed,
        out_specs=(P("replica", None, "tensor"), P(None, "tensor")),
        check_vma=False,
    )
```
